32 devices in a mesh: dp: 16 (over z, y, x), tensor: 2 (over core).
Axes of the slice: x: 2, y: 2, z: 4, core: 2. Of those that a mesh axis runs over, the one named last changes fastest.
Arguments:
- tokens: bfloat16 [2048, 8192], P('dp', 'tensor'), may hold values from -6 to 6
- hidden_grad: bfloat16 [2048, 28672], P('dp', 'tensor'), may hold values from -0.125 to 0.125
- masters: float32 [2, 64, 128, 128], P('tensor', 'dp'), may hold values from -0.5 to 0.5
- block_row: int32 [2, 32], P('tensor'), may hold values from 0 to 63, as said below
- block_col: int32 [2, 32], P('tensor'), may hold values from 0 to 111
- owners: int32 [2, 64], P('tensor'), may hold values from 0 to 15, as said below
Outputs:
- grads: float32 [2, 192, 128, 128], P('tensor', 'dp')
The draws below stay inside these ranges and needn't reach their ends.
Inputs may be any that keep to these rules, and one draw needn't show every extreme that they name: `block_row`: in each slice the kept places are distinct. `owners`: in each slice every owner takes at most 12 of the 64 kept blocks, and some owner takes exactly 12.
All inputs are finite; a program needn't handle non-finite values.
Results may differ from the reference program's by a relative error of at most 0.0044.
Values may be sent and summed in bfloat16 or wider, within the bound.
No kernel may reach another device: no remote copies, remote signals or barrier semaphores. Data moves between devices by JAX's collectives and lax.ppermute only.
A program may use at most 64 MiB of HBM per device.

```python
import jax
import jax.numpy as jnp
from jax import lax

D = 8192
FF = 28672
B = 128
KP = 32
TOKENS = 2048
SLICES = 2
OWNERS = 16
KB2 = 64
CAP = 12
NRB = 64
NCB = 112


def place_blocks(key):

    def one_slice(slice_key):
        key_a, key_b, key_c, key_d = jax.random.split(slice_key, 4)
        column_order = jax.random.permutation(key_a, NCB).astype(jnp.int32)
        position = jnp.arange(KP, dtype=jnp.int32)
        column_index = jnp.take(column_order, position % NCB).astype(jnp.int32)
        first_rows = jax.random.randint(key_b, (KP,), 0, NRB, dtype=jnp.int32)
        marked = jax.random.randint(key_c, (), 0, min(KP, NCB), dtype=jnp.int32)
        first_rows = jnp.where(position == marked, NRB - 1, first_rows).astype(jnp.int32)
        offsets = jax.random.randint(key_d, (KP,), 1, NRB, dtype=jnp.int32)
        partner = jnp.take(first_rows, jnp.maximum(position - NCB, 0))
        row_index = jnp.where(position < NCB, first_rows, (partner + offsets) % NRB).astype(jnp.int32)
        return (row_index, column_index)
    return jax.vmap(one_slice)(jax.random.split(key, SLICES))


def draw_block_row(key, part):
    return place_blocks(jax.random.fold_in(key, 11))[0]


def draw_block_col(key, part):
    return place_blocks(jax.random.fold_in(key, 11))[1]


def draw_owners(key, part):

    def one_slice(slice_key):
        key_a, key_b, key_c = jax.random.split(slice_key, 3)
        full_owner = jax.random.randint(key_a, (), 0, OWNERS, dtype=jnp.int32)
        others = jax.random.permutation(key_b, (OWNERS - 1) * CAP)[:KB2 - CAP].astype(jnp.int32)
        others = jnp.where(others >= full_owner * CAP, others + CAP, others).astype(jnp.int32)
        slot_list = jnp.concatenate([full_owner * CAP + jnp.arange(CAP, dtype=jnp.int32), others])
        shuffled = jax.random.permutation(key_c, slot_list)
        return (shuffled // CAP).astype(jnp.int32)
    return jax.vmap(one_slice)(jax.random.split(jax.random.fold_in(key, 23), SLICES))


def steps_of(stream_key, shape, pieces, least, top_value):
    level, own = 1.0, jax.random.fold_in(stream_key, 6)
    for dim, shards_of in pieces:
        heights = jnp.exp(jax.random.uniform(jax.random.fold_in(own, dim), (shards_of,), jnp.float32, least / len(pieces), top_value / len(pieces)))
        level = level * jnp.repeat(heights, shape[dim] // shards_of).reshape([-1 if axis == dim else 1 for axis in range(len(shape))])
    return level


def bell_draw(rng, dims, deviation, limit, cuts=(), kind=jnp.bfloat16):
    level = steps_of(rng, dims, cuts, -0.22, 0.18) if cuts else 1.0
    values = jax.random.normal(rng, dims, jnp.float32) * deviation * level
    return jnp.minimum(jnp.maximum(values, -limit), limit).astype(kind)


def setup_inputs(seed: int = 0) -> dict:
    key_list = jax.random.split(jax.random.key(seed), 7)
    tokens = bell_draw(key_list[0], (TOKENS, D), 1.0, 6.0, ((0, 16), (1, 2)))
    hidden_grad = bell_draw(key_list[1], (TOKENS, FF), TOKENS ** -0.5, 0.125, ((0, 16), (1, 2)))
    masters = bell_draw(key_list[2], (SLICES, KB2, B, B), B ** -0.5, 0.5, ((0, 2), (1, 16)), jnp.float32)
    block_row = draw_block_row(jax.random.fold_in(key_list[6], 71), 0)
    block_col = draw_block_col(jax.random.fold_in(key_list[6], 71), 0)
    owners = draw_owners(jax.random.fold_in(key_list[6], 71), 0)
    return dict(tokens=tokens, hidden_grad=hidden_grad, masters=masters, block_row=block_row, block_col=block_col, owners=owners)


def slot_index(owner_row, capacity):
    count_all = owner_row.shape[0]
    same_owner = owner_row[:, None] == owner_row[None, :]
    earlier = jnp.arange(count_all, dtype=jnp.int32)[None, :] < jnp.arange(count_all, dtype=jnp.int32)[:, None]
    rank_index = jnp.sum(jnp.logical_and(same_owner, earlier).astype(jnp.int32), axis=1, dtype=jnp.int32)
    return owner_row * capacity + rank_index


def one_slice(tokens, grad_slice, weights, row_index, column_index):
    token_count = tokens.shape[0]
    high = lax.Precision.HIGHEST
    by_block = tokens.reshape(token_count, NRB, B)
    selected = jnp.take(by_block, row_index, axis=1).astype(jnp.float32)
    gate_part = jnp.einsum("tkb,kbc->ktc", selected, weights[:KP].astype(jnp.float32), precision=high)
    up_part = jnp.einsum("tkb,kbc->ktc", selected, weights[KP:].astype(jnp.float32), precision=high)
    gate_cols = jax.ops.segment_sum(gate_part, column_index, num_segments=NCB)
    up_cols = jax.ops.segment_sum(up_part, column_index, num_segments=NCB)
    grad_cols = jnp.moveaxis(grad_slice.reshape(token_count, NCB, B), 1, 0).astype(jnp.float32)
    sigmoid_gate = jax.nn.sigmoid(gate_cols)
    gate_grad = (grad_cols * up_cols * sigmoid_gate * (1.0 + gate_cols * (1.0 - sigmoid_gate))).astype(jnp.bfloat16)
    up_grad = (grad_cols * gate_cols * sigmoid_gate).astype(jnp.bfloat16)
    gate_blocks = jnp.take(gate_grad, column_index, axis=0).astype(jnp.float32)
    up_blocks = jnp.take(up_grad, column_index, axis=0).astype(jnp.float32)
    grad_gate = jnp.einsum("tkb,ktc->kbc", selected, gate_blocks, precision=high)
    grad_up = jnp.einsum("tkb,ktc->kbc", selected, up_blocks, precision=high)
    return jnp.concatenate([grad_gate, grad_up], axis=0)


def reference(tokens, hidden_grad, masters, block_row, block_col, owners):
    weights = masters.astype(jnp.bfloat16)
    slice_width = FF // SLICES

    def per_slice(slice_number):
        grad_slice = lax.dynamic_slice_in_dim(hidden_grad, slice_number * slice_width, slice_width, 1)
        return one_slice(tokens, grad_slice, weights[slice_number], block_row[slice_number], block_col[slice_number])

    block_grads = lax.map(per_slice, jnp.arange(SLICES, dtype=jnp.int32))
    slot_list = jax.vmap(lambda owner_row: slot_index(owner_row, CAP))(owners)
    result = jnp.zeros((SLICES, OWNERS * CAP, B, B), jnp.float32)
    slice_numbers = jnp.arange(SLICES, dtype=jnp.int32)[:, None]
    return result.at[slice_numbers, slot_list].set(block_grads)
```

```python
import functools

import jax
import jax.numpy as jnp
import numpy as np
from jax import lax
from jax.experimental import pallas as pl
from jax.experimental.pallas import tpu as pltpu
from jax.sharding import PartitionSpec as P

VMEM = pl.BlockSpec(memory_space=pltpu.VMEM)
SMEM = pl.BlockSpec(memory_space=pltpu.SMEM)
BF16 = jnp.bfloat16
F32 = jnp.float32


def call(body, name, outs, in_specs, args, flops=0, scratch=()):
    moved = sum(int(np.prod(o.shape)) * o.dtype.itemsize for o in outs)
    moved += sum(int(np.prod(a.shape)) * a.dtype.itemsize for a in args)
    return pl.pallas_call(
        body,
        name=name,
        out_shape=tuple(outs),
        in_specs=in_specs,
        out_specs=tuple(VMEM for _ in outs),
        scratch_shapes=list(scratch),
        compiler_params=pltpu.CompilerParams(vmem_limit_bytes=40 << 20),
        cost_estimate=pl.CostEstimate(flops=flops, bytes_accessed=moved, transcendentals=0),
    )(*args)


def swap(value, axis, bit):
    size = lax.axis_size(axis)
    return lax.ppermute(value, axis, [(i, i ^ (1 << bit)) for i in range(size)])


def spread(value):
    parts = [value[None]]
    for bit in range(lax.axis_size("tensor").bit_length() - 1):
        whole = parts[0] if len(parts) == 1 else jnp.concatenate(parts, 0)
        parts.append(swap(whole, "tensor", bit))
    return parts


def split_masters(place, masters, kept, sent):
    half = kept.shape[1]
    for block in range(masters.shape[1]):
        turned = masters[0, block].T.astype(BF16)

        @pl.when(place[0] == 0)
        def _():
            kept[block] = turned[:half]
            sent[block] = turned[half:]

        @pl.when(place[0] != 0)
        def _():
            kept[block] = turned[half:]
            sent[block] = turned[:half]


def split_upstream(place, column, grad, kept, sent):
    count, half, side = kept.shape[0], kept.shape[1], kept.shape[2]

    def step(k, _):
        start = pl.multiple_of(column[0, k] * side, side)
        turned = grad[:, pl.ds(start, side)].T

        @pl.when(place[0] == 0)
        def _():
            kept[k] = turned[:half]
            sent[k] = turned[half:]

        @pl.when(place[0] != 0)
        def _():
            kept[k] = turned[half:]
            sent[k] = turned[:half]

        return 0

    lax.fori_loop(0, count, step, 0)


def select_rows(place, row, *refs):
    sources, chosen = refs[:-1], refs[-1]
    side = chosen.shape[2]
    per_shard = sources[0].shape[2] // side

    def step(k, _):
        shard = row[0, k] // per_shard
        start = pl.multiple_of((row[0, k] - shard * per_shard) * side, side)
        offset = shard ^ place[1]
        first = 0
        for source in sources:
            size = source.shape[0]

            @pl.when(jnp.logical_and(offset >= first, offset < first + size))
            def _():
                chosen[k] = source[offset - first, :, pl.ds(start, side)]

            first += size
        return 0

    lax.fori_loop(0, chosen.shape[0], step, 0)


def put(value, dst, sent, kept):
    @pl.when(dst >= 0)
    def _():
        sent[dst] = value.astype(BF16)

    @pl.when(dst < 0)
    def _():
        kept[-1 - dst] = value


def gradients(rows, table, *refs):
    (
        weight_a0, weight_a1, weight_b0, weight_b1, own_tokens, other_tokens, own_up, other_up,
        sent_a, kept_a, sent_b, kept_b, weights, total,
    ) = refs
    places, half = own_up.shape[0], own_up.shape[1]
    quarter = half // 2
    block_count = 2 * places
    tokens = own_tokens.shape[1]

    position = 0
    for source in (weight_a0, weight_a1, weight_b0, weight_b1):

        def order(p, _, source=source, position=position):
            block = table[rows["order"], position + p]
            up = (block >= places).astype(jnp.int32)
            start = pl.multiple_of(up * half, half)
            weights[block - up * places, pl.ds(start, half), :] = source[p]
            return 0

        lax.fori_loop(0, source.shape[0], order, 0, unroll=4)
        position += source.shape[0]

    contract_last = (((1,), (1,)), ((), ()))

    def forward(k, _):
        first = table[rows["first"], k]
        for n, source in enumerate((own_tokens, other_tokens)):
            part = lax.dot_general(weights[k], source[k], contract_last, preferred_element_type=F32)
            lanes = slice(n * tokens, (n + 1) * tokens)

            @pl.when(first == k)
            def _():
                total[k, :, lanes] = part

            @pl.when(first != k)
            def _():
                total[first, :, lanes] += part

        return 0

    lax.fori_loop(0, places, forward, 0)

    def backward(k, _):
        first = table[rows["first"], k]
        result = None
        for n, (source, upstream) in enumerate(((own_tokens, own_up), (other_tokens, other_up))):
            lanes = slice(n * tokens, (n + 1) * tokens)
            gate = total[first, :half, lanes]
            up = total[first, half:, lanes]
            sigmoid = 0.5 + 0.5 * jnp.tanh(0.5 * gate)
            scaled = upstream[k].astype(F32) * sigmoid
            gate_grad = scaled * up * (1.0 + gate * (1.0 - sigmoid))
            up_grad = scaled * gate
            both = jnp.concatenate([gate_grad.astype(BF16), up_grad.astype(BF16)], axis=0)
            term = jnp.dot(both, source[k], preferred_element_type=F32)
            result = term if result is None else result + term
        for which in range(2):
            block = k + which * places
            start = which * half
            put(result[start : start + quarter], table[rows["a"], block], sent_a, kept_a)
            put(result[start + quarter : start + half], table[rows["b"], block], sent_b, kept_b)
        return 0

    lax.fori_loop(0, places, backward, 0)


def combine(row, count_at, pieces, table, *refs):
    kept_in, received, sent, kept = refs[:pieces], refs[pieces : 2 * pieces], refs[-2], refs[-1]

    def step(r, _):
        value = [kept_in[n][r] + received[n][r].astype(F32) for n in range(pieces)]
        put(value[0] if pieces == 1 else jnp.concatenate(value, 0), table[row, r], sent, kept)
        return 0

    lax.fori_loop(0, table[count_at[0], count_at[1]], step, 0)


def finish(count_at, place, table, kept, received, out):
    count = table[count_at[0], count_at[1]]
    for slot in range(out.shape[1]):

        @pl.when(slot < count)
        def _():
            mine, other = kept[slot], received[slot].astype(F32)
            swapped = place[0] != 0
            low = jnp.where(swapped, other, mine)
            high = jnp.where(swapped, mine, other)
            out[0, slot] = jnp.concatenate([low, high], axis=0).T

        @pl.when(slot >= count)
        def _():
            out[0, slot] = jnp.zeros(out.shape[2:], F32)


def axes_of(owner_count):
    bits = owner_count.bit_length() - 1
    if bits == 4:
        return 2, (0, 1), (3,)
    return 0, (bits - 1, 1), tuple(b for b in range(2, bits - 1))


def rank(mask):
    count = mask.shape[0]
    earlier = np.tril(np.ones((count, count), bool), -1)
    return jnp.sum(jnp.logical_and(mask[None, :], earlier).astype(jnp.int32), axis=1, dtype=jnp.int32)


def plan(owner, column, me, order, bits):
    pair, (bit_a, bit_b), rest = bits
    block_count = owner.shape[0]
    differs = owner ^ me

    def alive(done):
        return (differs & sum(1 << b for b in done)) == 0

    def target(done, bit):
        live, away = alive(done), ((differs >> bit) & 1) == 1
        send, keep = jnp.logical_and(live, away), jnp.logical_and(live, jnp.logical_not(away))
        return jnp.where(send, rank(send), -1 - rank(keep))

    def listed(done, values):
        live = alive(done)
        place = rank(live)
        hit = jnp.logical_and(live[None, :], place[None, :] == np.arange(block_count)[:, None])
        return jnp.sum(jnp.where(hit, values[None, :], 0), axis=1, dtype=jnp.int32)

    rows, table, counts = {}, [], {}

    def add(name, values):
        rows[name] = len(table)
        table.append(jnp.pad(values.astype(jnp.int32), (0, block_count - values.shape[0])))

    def add_count(name, done):
        counts[name] = (-1, len(counts)), jnp.sum(alive(done).astype(jnp.int32), dtype=jnp.int32)

    add("order", order)
    places = column.shape[0]
    same = column[:, None] == column[None, :]
    add("first", jnp.min(jnp.where(same, np.arange(places, dtype=np.int32)[None, :], places), axis=1))
    add("a", target((), bit_a))
    add("b", target((), bit_b))
    steps = [("a2", (bit_a,), bit_b), ("b2", (bit_b,), bit_a)]
    done = (bit_a, bit_b)
    for bit in (*rest, pair):
        steps.append((f"s{len(done)}", done, bit))
        done = (*done, bit)
    for name, before, bit in steps:
        add(name, listed(before, target(before, bit)))
        add_count(name, before)
    add_count("end", done)
    last = len(table)
    table.append(jnp.pad(jnp.stack([c for _, c in counts.values()]), (0, block_count - len(counts))))
    return rows, {n: (last, at[1]) for n, (at, _) in counts.items()}, jnp.stack(table), steps


def most(owner, done):
    group = owner & sum(1 << b for b in done)
    return jnp.max(jnp.sum((group[:, None] == group[None, :]).astype(jnp.int32), axis=1, dtype=jnp.int32))


def local(tokens, hidden_grad, masters, block_row, block_col, owners):
    owner_count = lax.axis_size("dp")
    me = lax.axis_index("dp")
    bits = axes_of(owner_count)
    pair, (bit_a, bit_b), rest = bits
    own_blocks, side = masters.shape[1], masters.shape[2]
    places, half, quarter = block_row.shape[1], side // 2, side // 4
    block_count = owners.shape[1]
    token_count = tokens.shape[0]
    capacity = 3 * block_count // owner_count
    place = jnp.stack([(me >> pair) & 1, lax.axis_index("tensor")]).astype(jnp.int32)

    def struct(shape, dtype):
        return jax.ShapeDtypeStruct(shape, dtype)

    with jax.named_scope("weights"):
        kept, sent = call(
            split_masters, "split_masters", [struct((own_blocks, half, side), BF16)] * 2, [SMEM, VMEM], [place, masters]
        )
        entries = [(0, b) for b in range(own_blocks)]

        def moved(bit):
            return [(delta ^ (1 << bit), b) for delta, b in entries]

        current = jnp.concatenate([kept, swap(sent, "dp", pair)], 0)
        entries += moved(pair)
        for bit in rest[:0:-1]:
            current = jnp.concatenate([current, swap(current, "dp", bit)], 0)
            entries += moved(bit)
        base, first_part = entries, current
        second_part = swap(current, "dp", rest[0])
        entries = base
        a0 = jnp.concatenate([first_part, swap(first_part, "dp", bit_a)], 0)
        entries_a = base + moved(bit_a)
        entries = entries_a
        entries_a = entries_a + moved(bit_b)
        entries = base
        base_b = moved(rest[0])
        entries = base_b
        entries_b = base_b + moved(bit_b)
        entries = entries_b
        entries_b = entries_b + moved(bit_a)
        b0 = jnp.concatenate([second_part, swap(second_part, "dp", bit_b)], 0)
        a1, b1 = swap(a0, "dp", bit_b), swap(b0, "dp", bit_a)
        found = entries_a + entries_b
        order = (me ^ np.array([d for d, _ in found], np.int32)) * own_blocks + np.array([b for _, b in found], np.int32)

    with jax.named_scope("tokens"):
        other = swap(tokens, "dp", pair)
        chosen = [
            call(
                select_rows, "select_rows", [struct((places, token_count, side), BF16)],
                [SMEM, SMEM] + [VMEM] * len(parts), [place, block_row, *parts],
            )[0]
            for parts in (spread(tokens), spread(other))
        ]

    with jax.named_scope("upstream"):
        own_up, sent_up = call(
            split_upstream, "split_upstream", [struct((places, half, token_count), BF16)] * 2,
            [SMEM, SMEM, VMEM], [place, block_col, hidden_grad],
        )
        other_up = swap(sent_up, "dp", pair)

    with jax.named_scope("plan"):
        rows, count_at, table, steps = plan(owners[0], block_col[0], me, order, bits)

        def full(done):
            return min(block_count, (owner_count >> len(done)) * capacity)

        def usual(done):
            return min(full(done), (block_count >> len(done)) + capacity)

        fits = jnp.bool_(True)
        for _, done, _ in steps:
            if done and usual(done) < full(done):
                fits = jnp.logical_and(fits, most(owners[0], done) <= usual(done))
        fits = fits.astype(jnp.int32).reshape(1, 1)
        for bit in range(lax.axis_size("tensor").bit_length() - 1):
            fits = jnp.minimum(fits, swap(fits, "tensor", bit))

    def reduce(size, *args):
        (table, place, *inputs) = args
        outs = []
        for bit in (bit_a, bit_b):
            room = size((bit,))
            outs += [struct((room, quarter, side), BF16), struct((room, quarter, side), F32)]
        work = 2 * 2 * places * side * side * 2 * token_count
        sent_a, kept_a, sent_b, kept_b = call(
            functools.partial(gradients, rows), "gradients", outs, [SMEM] + [VMEM] * 8, [table, *inputs], work,
            [pltpu.VMEM((places, side, side), BF16), pltpu.VMEM((places, side, 2 * token_count), F32)],
        )

        def join(name, done, kept_in, received):
            pieces = len(kept_in)
            room, height = size(done), sum(k.shape[1] for k in kept_in)
            return call(
                functools.partial(combine, rows[name], count_at[name], pieces), "combine",
                [struct((room, height, side), BF16), struct((room, height, side), F32)],
                [SMEM] + [VMEM] * (2 * pieces), [table, *kept_in, *received],
            )

        got_a, got_b = swap(sent_a, "dp", bit_a), swap(sent_b, "dp", bit_b)
        both = (bit_a, bit_b)
        sent_a, kept_a = join("a2", both, [kept_a], [got_a])
        got_a = swap(sent_a, "dp", bit_b)
        sent_b, kept_b = join("b2", both, [kept_b], [got_b])
        got_b = swap(sent_b, "dp", bit_a)
        kept, got, done = [kept_a, kept_b], [got_a, got_b], both
        for name, _, bit in steps[2:]:
            done = (*done, bit)
            sent, held = join(name, done, kept, got)
            kept, got = [held], [swap(sent, "dp", bit)]
        return call(
            functools.partial(finish, count_at["end"]), "finish", [struct((1, capacity, side, side), F32)],
            [SMEM, SMEM, VMEM, VMEM], [place, table, kept[0], got[0]],
        )[0]

    operands = (table, place, a0, a1, b0, b1, *chosen, own_up, other_up)
    return lax.cond(
        fits[0, 0] == 1, functools.partial(reduce, usual), functools.partial(reduce, full), *operands
    )


def solution(mesh):
    return jax.shard_map(
        local,
        mesh=mesh,
        in_specs=(
            P("dp", "tensor"),
            P("dp", "tensor"),
            P("tensor", "dp", None, None),
            P("tensor", None),
            P("tensor", None),
            P("tensor", None),
        ),
        out_specs=P("tensor", "dp", None, None),
        check_vma=False,
    )
```

```python
import functools

import jax
import jax.numpy as jnp
import numpy as np
from jax import lax
from jax.experimental import pallas as pl
from jax.experimental.pallas import tpu as pltpu
from jax.sharding import PartitionSpec as P

VMEM = pl.BlockSpec(memory_space=pltpu.VMEM)
SMEM = pl.BlockSpec(memory_space=pltpu.SMEM)
BF16 = jnp.bfloat16
F32 = jnp.float32


def call(body, name, outs, in_specs, args, flops=0, scratch=()):
    moved = sum(int(np.prod(o.shape)) * o.dtype.itemsize for o in outs)
    moved += sum(int(np.prod(a.shape)) * a.dtype.itemsize for a in args)
    return pl.pallas_call(
        body,
        name=name,
        out_shape=tuple(outs),
        in_specs=in_specs,
        out_specs=tuple(VMEM for _ in outs),
        scratch_shapes=list(scratch),
        compiler_params=pltpu.CompilerParams(vmem_limit_bytes=40 << 20),
        cost_estimate=pl.CostEstimate(flops=flops, bytes_accessed=moved, transcendentals=0),
    )(*args)


def swap(value, axis, bit):
    size = lax.axis_size(axis)
    return lax.ppermute(value, axis, [(i, i ^ (1 << bit)) for i in range(size)])


def spread(value):
    parts = [value[None]]
    for bit in range(lax.axis_size("tensor").bit_length() - 1):
        whole = parts[0] if len(parts) == 1 else jnp.concatenate(parts, 0)
        parts.append(swap(whole, "tensor", bit))
    return parts


def split_masters(place, masters, kept, sent):
    half = kept.shape[1]
    for block in range(masters.shape[1]):
        turned = masters[0, block].T.astype(BF16)

        @pl.when(place[0] == 0)
        def _():
            kept[block] = turned[:half]
            sent[block] = turned[half:]

        @pl.when(place[0] != 0)
        def _():
            kept[block] = turned[half:]
            sent[block] = turned[:half]


def split_upstream(place, column, grad, kept, sent, blocks, arrived):
    count, half, side = kept.shape[0], kept.shape[1], kept.shape[2]

    def fetch(k):
        start = pl.multiple_of(column[0, k] * side, side)
        return pltpu.make_async_copy(grad.at[:, pl.ds(start, side)], blocks.at[k], arrived.at[k])

    for k in range(count):
        fetch(k).start()
    for k in range(count):
        fetch(k).wait()
        turned = blocks[k].T
        low, high = turned[:half], turned[half:]
        swapped = place[0] != 0
        kept[k] = jnp.where(swapped, high, low)
        sent[k] = jnp.where(swapped, low, high)


def select(place, row, sources, k, side):
    per_shard = sources[0].shape[2] // side
    shard = row[0, k] // per_shard
    start = pl.multiple_of((row[0, k] - shard * per_shard) * side, side)
    offset = shard ^ place[1]
    value, first = None, 0
    for source in sources:
        size = source.shape[0]
        here = source[jnp.clip(offset - first, 0, size - 1), :, pl.ds(start, side)]
        value = here if value is None else jnp.where(offset >= first, here, value)
        first += size
    return value


def select_rows(place, row, *refs):
    sources, chosen = refs[:-1], refs[-1]
    for k in range(chosen.shape[0]):
        chosen[k] = select(place, row, sources, k, chosen.shape[2])


def add_duplicates(first, table, total):
    for k in range(1, total.shape[0]):

        @pl.when(table[first, k] != k)
        def _():
            total[table[first, k]] += total[k]


def slopes(gate, up):
    sigmoid = 0.5 + 0.5 * jnp.tanh(0.5 * gate)
    return sigmoid * up * (1.0 + gate * (1.0 - sigmoid)), sigmoid * gate


def project(weight, source):
    return lax.dot_general(weight, source, (((1,), (1,)), ((), ())), preferred_element_type=F32)


def term(upstream, gate_slope, up_slope, source):
    upstream = upstream.astype(F32)
    both = [(upstream * gate_slope).astype(BF16), (upstream * up_slope).astype(BF16)]
    return jnp.dot(jnp.concatenate(both, axis=0), source, preferred_element_type=F32)


def own_part(rows, table, *refs):
    sources, own_tokens, own_up, weights, grad, total = refs[:4], refs[4], refs[5], refs[6], refs[7], refs[8]
    places, half = own_up.shape[0], own_up.shape[1]
    position = 0
    for source in sources:
        for p in range(source.shape[0]):
            block = table[rows["order"], position + p]
            up = (block >= places).astype(jnp.int32)
            weights[block - up * places, pl.ds(pl.multiple_of(up * half, half), half), :] = source[p]
        position += source.shape[0]
    for k in range(places):
        total[k] = project(weights[k], own_tokens[k])
    add_duplicates(rows["first"], table, total)
    for k in range(places):
        first = table[rows["first"], k]
        grad[k] = term(own_up[k], *slopes(total[first, :half], total[first, half:]), own_tokens[k])


def other_slopes(rows, table, place, row, weights, *refs):
    sources, chosen, slope, total = refs[:-3], refs[-3], refs[-2], refs[-1]
    places, half = weights.shape[0], weights.shape[1] // 2
    for k in range(places):
        value = select(place, row, sources, k, chosen.shape[2])
        chosen[k] = value
        total[k] = project(weights[k], value)
    add_duplicates(rows["first"], table, total)
    for k in range(places):
        first = table[rows["first"], k]
        slope[k, :half], slope[k, half:] = slopes(total[first, :half], total[first, half:])


def other_part(rows, table, slope, other_tokens, other_up, grad, sent_a, kept_a, sent_b, kept_b, total):
    places, half = other_up.shape[0], other_up.shape[1]
    quarter = half // 2
    for k in range(places):
        total[k] = grad[k] + term(other_up[k], slope[k, :half], slope[k, half:], other_tokens[k])
    for block in range(2 * places):
        which, k = divmod(block, places)
        for name, start, sent, kept in (("a", 0, sent_a, kept_a), ("b", quarter, sent_b, kept_b)):
            value = total[k, pl.ds(which * half + start, quarter), :]
            sent[table[rows[name + "_sent"], block]] = value.astype(BF16)
            kept[table[rows[name + "_kept"], block]] = value


def combine(sent_row, kept_row, pieces, table, *refs):
    kept_in, received, sent, kept = refs[:pieces], refs[pieces : 2 * pieces], refs[-2], refs[-1]
    room = sent.shape[0]
    for r in range(kept_in[0].shape[0]):
        value = [kept_in[n][r] + received[n][r].astype(F32) for n in range(pieces)]
        value = value[0] if pieces == 1 else jnp.concatenate(value, 0)
        sent[jnp.minimum(table[sent_row, r], room - 1)] = value.astype(BF16)
        kept[jnp.minimum(table[kept_row, r], room - 1)] = value


def combine_last(sent_row, kept_row, count_row, table, kept_in, received, sent, kept):
    def step(r, _):
        value = kept_in[r] + received[r].astype(F32)
        away = table[sent_row, r]

        @pl.when(away >= 0)
        def _():
            sent[away] = value.astype(BF16)

        @pl.when(away < 0)
        def _():
            kept[table[kept_row, r]] = value

        return 0

    lax.fori_loop(0, table[count_row, 0], step, 0)


def finish(count_row, place, table, kept, received, out):
    count = table[count_row, 0]
    for slot in range(out.shape[1]):

        @pl.when(slot < count)
        def _():
            mine, other = kept[slot], received[slot].astype(F32)
            swapped = place[0] != 0
            low = jnp.where(swapped, other, mine)
            high = jnp.where(swapped, mine, other)
            out[0, slot] = jnp.concatenate([low, high], axis=0).T

        @pl.when(slot >= count)
        def _():
            out[0, slot] = jnp.zeros(out.shape[2:], F32)


def axes_of(owner_count):
    bits = owner_count.bit_length() - 1
    if bits == 4:
        return 0, (1, 2), (3,)
    return bits - 2, (0, bits - 1), tuple(range(1, bits - 2))


def steps_of(bits):
    pair, (bit_a, bit_b), rest = bits
    steps = [("a2", (bit_a,), bit_b), ("b2", (bit_b,), bit_a)]
    done = (bit_a, bit_b)
    for bit in (*rest, pair):
        steps.append((f"s{len(done)}", done, bit))
        done = (*done, bit)
    return steps


def rows_of(bits):
    names = ["order", "first"]
    for name in ["a", "b"] + [name for name, _, _ in steps_of(bits)]:
        names += [name + "_sent", name + "_kept"]
    return {name: n for n, name in enumerate(names + ["last", "end", "fits"])}


def make_plan(bits, usual, own_blocks, place, owners, columns, found, table):
    pair, (bit_a, bit_b), _ = bits
    rows = rows_of(bits)
    count, places = owners.shape[1], columns.shape[1]
    me = place[2]
    across = lax.broadcasted_iota(jnp.int32, (count, count), 1)
    down = lax.broadcasted_iota(jnp.int32, (count, count), 0)
    owner_row, column_row = owners[...], columns[...]

    def as_column(row):
        size = row.shape[1]
        kept = jnp.where((across == down)[:size, :size], row.astype(F32), 0.0)
        return jnp.sum(kept, axis=1, keepdims=True).astype(jnp.int32)

    owner_col, column_col = as_column(owner_row), as_column(column_row)
    before = across < down
    differs_row, differs_col = owner_row ^ me, owner_col ^ me

    def alive(differs, done):
        return (differs & sum(1 << b for b in done)) == 0

    def number(mask):
        return jnp.where(mask, 1.0, 0.0)

    def rank(mask_row):
        return jnp.sum(jnp.where(before, number(mask_row), 0.0), axis=1, keepdims=True)

    def turned(column):
        return jnp.sum(jnp.where(across == down, column, 0.0), axis=0, keepdims=True)

    def write(name, row):
        table[pl.ds(rows[name], 1), :] = row.astype(jnp.int32)

    def going(done, bit):
        live, away = alive(differs_row, done), ((differs_row >> bit) & 1) == 1
        return rank(jnp.logical_and(live, away)), rank(jnp.logical_and(live, jnp.logical_not(away)))

    table[...] = jnp.zeros(table.shape, jnp.int32)
    table[pl.ds(rows["order"], 1), :] = (found[0:1, :] ^ me) * own_blocks + found[1:2, :]
    same = column_row == column_col
    place_at = lax.broadcasted_iota(jnp.int32, (places, places), 0).astype(F32)
    first = jnp.min(jnp.where(same, place_at, float(places)), axis=0, keepdims=True)
    table[pl.ds(rows["first"], 1), :places] = first.astype(jnp.int32)
    for name, bit in (("a", bit_a), ("b", bit_b)):
        sent, kept = going((), bit)
        write(name + "_sent", turned(sent))
        write(name + "_kept", turned(kept))
    full, at_most = float(count), None
    for name, done, bit in steps_of(bits):
        sent, kept = going(done, bit)
        live = rank(alive(differs_row, done))
        hit = jnp.logical_and(alive(differs_col, done), live == across.astype(F32))
        if bit == pair:
            sent = jnp.where(((differs_col >> bit) & 1) == 1, sent, -1.0)
        for kind, values in (("_sent", sent), ("_kept", kept)):
            write(name + kind, full + jnp.sum(jnp.where(hit, values - full, 0.0), axis=0, keepdims=True))
        if name in usual:
            mask = sum(1 << b for b in done)
            group = (owner_row & mask) == (owner_col & mask)
            over = jnp.max(jnp.sum(number(group), axis=1, keepdims=True), axis=0, keepdims=True) - usual[name]
            at_most = over if at_most is None else jnp.maximum(at_most, over)
    for name, done in (("last", done), ("end", (*done, pair))):
        total = jnp.sum(number(alive(differs_row, done)), axis=1, keepdims=True)
        write(name, jnp.broadcast_to(total, (1, count)))
    fits = jnp.zeros((1, 1), F32) if at_most is None else at_most
    write("fits", jnp.broadcast_to(number(fits <= 0.0), (1, count)))


def local(tokens, hidden_grad, masters, block_row, block_col, owners):
    owner_count = lax.axis_size("dp")
    me = lax.axis_index("dp")
    bits = axes_of(owner_count)
    pair, (bit_a, bit_b), rest = bits
    own_blocks, side = masters.shape[1], masters.shape[2]
    places, half, quarter = block_row.shape[1], side // 2, side // 4
    block_count = owners.shape[1]
    token_count = tokens.shape[0]
    capacity = 3 * block_count // owner_count
    place = jnp.stack([(me >> pair) & 1, lax.axis_index("tensor"), me]).astype(jnp.int32)

    def struct(shape, dtype):
        return jax.ShapeDtypeStruct(shape, dtype)

    with jax.named_scope("weights"):
        kept, sent = call(
            split_masters, "split_masters", [struct((own_blocks, half, side), BF16)] * 2, [SMEM, VMEM], [place, masters]
        )
        entries = [(0, b) for b in range(own_blocks)]

        def moved(found, bit):
            return [(delta ^ (1 << bit), b) for delta, b in found]

        got = swap(sent, "dp", pair)
        entries = entries + moved(entries, pair)
        tokens, hidden_grad, owners, got = lax.optimization_barrier((tokens, hidden_grad, owners, got))
        current = jnp.concatenate([kept, got], 0)
        for bit in rest[:0:-1]:
            current = jnp.concatenate([current, swap(current, "dp", bit)], 0)
            entries = entries + moved(entries, bit)
        far = swap(current, "dp", rest[0])
        own_up, sent_up = call(
            split_upstream, "split_upstream", [struct((places, half, token_count), BF16)] * 2,
            [SMEM, SMEM, pl.BlockSpec(memory_space=pl.ANY)], [place, block_col, hidden_grad], 0,
            [pltpu.VMEM((places, token_count, side), BF16), pltpu.SemaphoreType.DMA((places,))],
        )
        current, far, sent_up = lax.optimization_barrier((current, far, sent_up))
        a0 = jnp.concatenate([current, swap(current, "dp", bit_a)], 0)
        b0 = jnp.concatenate([far, swap(far, "dp", bit_b)], 0)
        entries_a, entries_b = entries + moved(entries, bit_a), moved(entries, rest[0])
        entries_b = entries_b + moved(entries_b, bit_b)
        a1, b1 = swap(a0, "dp", bit_b), swap(b0, "dp", bit_a)
        found = entries_a + moved(entries_a, bit_b) + entries_b + moved(entries_b, bit_a)
        found = np.array(found, np.int32).T

    with jax.named_scope("plan"):

        def most_of(done):
            return min(block_count, (owner_count >> len(done)) * capacity)

        def load_of(done):
            return min(most_of(done), (block_count >> len(done)) + capacity)

        rows, steps = rows_of(bits), steps_of(bits)
        usual = {name: load_of(done) for name, done, _ in steps if load_of(done) < most_of(done)}
        table = call(
            functools.partial(make_plan, bits, usual, own_blocks), "make_plan",
            [struct((-(-len(rows) // 8) * 8, block_count), jnp.int32)], [SMEM] + [VMEM] * 3,
            [place, owners, block_col, jnp.asarray(found)],
        )[0]
        fits = table[rows["fits"], :1]
        for bit in range(lax.axis_size("tensor").bit_length() - 1):
            fits = jnp.minimum(fits, swap(fits, "tensor", bit))

    with jax.named_scope("tokens"):
        other = swap(tokens, "dp", pair)
        parts = spread(tokens)
        own_chosen = call(
            select_rows, "select_rows", [struct((places, token_count, side), BF16)],
            [SMEM, SMEM] + [VMEM] * len(parts), [place, block_row, *parts],
        )[0]
        other, _ = lax.optimization_barrier((other, (a1, b1)))
        other_parts = spread(other)

    with jax.named_scope("upstream"):
        other_up = swap(sent_up, "dp", pair)

    work = 2 * 2 * places * side * side * token_count
    with jax.named_scope("own_tokens"):
        weights, grad = call(
            functools.partial(own_part, rows), "own_part",
            [struct((places, side, side), BF16), struct((places, side, side), F32)], [SMEM] + [VMEM] * 6,
            [table, a0, a1, b0, b1, own_chosen, own_up], work, [pltpu.VMEM((places, side, token_count), F32)],
        )
    with jax.named_scope("other_tokens"):
        other_chosen, slope = call(
            functools.partial(other_slopes, rows), "other_slopes",
            [struct((places, token_count, side), BF16), struct((places, side, token_count), F32)],
            [SMEM] * 3 + [VMEM] * (1 + len(other_parts)), [table, place, block_row, weights, *other_parts], work // 2,
            [pltpu.VMEM((places, side, token_count), F32)],
        )

    def reduce(load, table, slope, other_chosen, other_up, grad):
        outs = []
        for bit in (bit_a, bit_b):
            room = load((bit,)) + 1
            outs += [struct((room, quarter, side), BF16), struct((room, quarter, side), F32)]
        sent_a, kept_a, sent_b, kept_b = call(
            functools.partial(other_part, rows), "other_part", outs, [SMEM] + [VMEM] * 4,
            [table, slope, other_chosen, other_up, grad], work // 2, [pltpu.VMEM((places, side, side), F32)],
        )

        def join(name, done, kept_in, received):
            pieces = len(kept_in)
            at = rows[name + "_sent"], rows[name + "_kept"]
            if done[-1] == pair:
                body, room = functools.partial(combine_last, *at, rows["last"]), capacity
            else:
                body, room = functools.partial(combine, *at, pieces), load(done) + 1
            height = sum(k.shape[1] for k in kept_in)
            return call(
                body, "combine", [struct((room, height, side), BF16), struct((room, height, side), F32)],
                [SMEM] + [VMEM] * (2 * pieces), [table, *kept_in, *received],
            )

        got_a, got_b = swap(sent_a, "dp", bit_a), swap(sent_b, "dp", bit_b)
        both = (bit_a, bit_b)
        sent_a, kept_a = join("a2", both, [kept_a], [got_a])
        got_a = swap(sent_a, "dp", bit_b)
        sent_b, kept_b = join("b2", both, [kept_b], [got_b])
        got_b = swap(sent_b, "dp", bit_a)
        kept, got, done = [kept_a, kept_b], [got_a, got_b], both
        for name, _, bit in steps[2:]:
            done = (*done, bit)
            sent, held = join(name, done, kept, got)
            kept, got = [held], [swap(sent, "dp", bit)]
        return kept[0], got[0]

    operands = (table, slope, other_chosen, other_up, grad)
    kept, got = lax.cond(
        fits[0] == 1, functools.partial(reduce, load_of), functools.partial(reduce, most_of), *operands
    )
    return call(
        functools.partial(finish, rows["end"]), "finish", [struct((1, capacity, side, side), F32)],
        [SMEM, SMEM, VMEM, VMEM], [place, table, kept, got],
    )[0]


def solution(mesh):
    return jax.shard_map(
        local,
        mesh=mesh,
        in_specs=(
            P("dp", "tensor"),
            P("dp", "tensor"),
            P("tensor", "dp", None, None),
            P("tensor", None),
            P("tensor", None),
            P("tensor", None),
        ),
        out_specs=P("tensor", "dp", None, None),
        check_vma=False,
    )
```

```python
import functools

import jax
import jax.numpy as jnp
import numpy as np
from jax import lax
from jax.experimental import pallas as pl
from jax.experimental.pallas import tpu as pltpu
from jax.sharding import PartitionSpec as P

VMEM = pl.BlockSpec(memory_space=pltpu.VMEM)
SMEM = pl.BlockSpec(memory_space=pltpu.SMEM)
BF16 = jnp.bfloat16
F32 = jnp.float32


def call(body, name, outs, in_specs, args, flops=0, scratch=()):
    moved = sum(int(np.prod(o.shape)) * o.dtype.itemsize for o in outs)
    moved += sum(int(np.prod(a.shape)) * a.dtype.itemsize for a in args)
    return pl.pallas_call(
        body,
        name=name,
        out_shape=tuple(outs),
        in_specs=in_specs,
        out_specs=tuple(VMEM for _ in outs),
        scratch_shapes=list(scratch),
        compiler_params=pltpu.CompilerParams(vmem_limit_bytes=40 << 20),
        cost_estimate=pl.CostEstimate(flops=flops, bytes_accessed=moved, transcendentals=0),
    )(*args)


def swap(value, axis, bit):
    size = lax.axis_size(axis)
    return lax.ppermute(value, axis, [(i, i ^ (1 << bit)) for i in range(size)])


def spread(value):
    parts = [value[None]]
    for bit in range(lax.axis_size("tensor").bit_length() - 1):
        whole = parts[0] if len(parts) == 1 else jnp.concatenate(parts, 0)
        parts.append(swap(whole, "tensor", bit))
    return parts


def split_masters(place, masters, kept, sent):
    half = kept.shape[1]
    for block in range(masters.shape[1]):
        turned = masters[0, block].T.astype(BF16)

        @pl.when(place[0] == 0)
        def _():
            kept[block] = turned[:half]
            sent[block] = turned[half:]

        @pl.when(place[0] != 0)
        def _():
            kept[block] = turned[half:]
            sent[block] = turned[:half]


def split_upstream(place, grad, kept, *refs):
    parts, blocks, arrived = refs[:-2], refs[-2], refs[-1]
    count, half, side = kept.shape[0], kept.shape[1], kept.shape[2]

    def fetch(k):
        start = pl.multiple_of(place[3 + count + k] * side, side)
        return pltpu.make_async_copy(grad.at[:, pl.ds(start, side)], blocks.at[k], arrived.at[k])

    for k in range(count):
        fetch(k).start()
    for k in range(count):
        fetch(k).wait()
        turned = blocks[k].T
        low, high = turned[:half], turned[half:]
        swapped = place[0] != 0
        kept[k] = jnp.where(swapped, high, low)
        sent = jnp.where(swapped, low, high)
        start = 0
        for part in parts:
            part[k] = sent[start : start + part.shape[1]]
            start += part.shape[1]


def select_rows(first, place, *refs):
    sources, before, chosen = refs[: 1 if first == 0 else -2], refs[-2], refs[-1]
    side = chosen.shape[2]
    per_shard = sources[0].shape[2] // side
    for k in range(chosen.shape[0]):
        shard = place[3 + k] // per_shard
        start = pl.multiple_of((place[3 + k] - shard * per_shard) * side, side)
        offset = shard ^ place[1]
        value, at = None if first == 0 else before[k], first
        for source in sources:
            size = source.shape[0]
            here = source[jnp.clip(offset - at, 0, size - 1), :, pl.ds(start, side)]
            value = here if value is None else jnp.where(offset >= at, here, value)
            at += size
        chosen[k] = value


def add_duplicates(first, table, total):
    for k in range(1, total.shape[0]):

        @pl.when(table[first, k] != k)
        def _():
            total[table[first, k]] += total[k]


def slopes(gate, up):
    sigmoid = 0.5 + 0.5 * jnp.tanh(0.5 * gate)
    return sigmoid * up * (1.0 + gate * (1.0 - sigmoid)), sigmoid * gate


def project(weight, source):
    return lax.dot_general(weight, source, (((1,), (1,)), ((), ())), preferred_element_type=F32)


def term(upstream, gate_slope, up_slope, source):
    upstream = upstream.astype(F32)
    both = [(upstream * gate_slope).astype(BF16), (upstream * up_slope).astype(BF16)]
    return jnp.dot(jnp.concatenate(both, axis=0), source, preferred_element_type=F32)


def own_part(rows, table, *refs):
    sources, own_tokens, own_up, weights, grad, total = refs[:4], refs[4], refs[5], refs[6], refs[7], refs[8]
    places, half = own_up.shape[0], own_up.shape[1]
    position = 0
    for source in sources:
        for p in range(source.shape[0]):
            block = table[rows["order"], position + p]
            up = (block >= places).astype(jnp.int32)
            weights[block - up * places, pl.ds(pl.multiple_of(up * half, half), half), :] = source[p]
        position += source.shape[0]
    for k in range(places):
        total[k] = project(weights[k], own_tokens[k])
    add_duplicates(rows["first"], table, total)
    for k in range(places):
        first = table[rows["first"], k]
        grad[k] = term(own_up[k], *slopes(total[first, :half], total[first, half:]), own_tokens[k])


def other_slopes(rows, table, weights, other_tokens, slope, total):
    places, half = weights.shape[0], weights.shape[1] // 2
    for k in range(places):
        total[k] = project(weights[k], other_tokens[k])
    add_duplicates(rows["first"], table, total)
    for k in range(places):
        first = table[rows["first"], k]
        slope[k, :half], slope[k, half:] = slopes(total[first, :half], total[first, half:])


def other_part(rows, names, start, table, slope, other_tokens, other_up, grad, *refs):
    outs, total = refs[:-1], refs[-1]
    places, height, half = other_up.shape[0], other_up.shape[1], grad.shape[1] // 2
    gate, up = pl.ds(start, height), pl.ds(half + start, height)
    for k in range(places):
        result = term(other_up[k], slope[k, gate], slope[k, up], other_tokens[k])
        total[k, :height] = grad[k, gate] + result[:height]
        total[k, height:] = grad[k, up] + result[height:]
    first = 0
    for n, name in enumerate(names):
        sent, kept = outs[2 * n], outs[2 * n + 1]
        room, size = sent.shape[0], sent.shape[1]
        for block in range(2 * places):
            which, k = divmod(block, places)
            value = total[k, pl.ds(which * height + first, size), :]
            sent[jnp.minimum(table[rows[name, "sent"], block], room - 1)] = value.astype(BF16)
            kept[jnp.minimum(table[rows[name, "kept"], block], room - 1)] = value
        first += size


def combine(sent_row, kept_row, table, kept_in, received, sent, kept):
    room = sent.shape[0]
    for r in range(kept_in.shape[0] - 1):
        value = kept_in[r] + received[r].astype(F32)
        sent[jnp.minimum(table[sent_row, r], room - 1)] = value.astype(BF16)
        kept[jnp.minimum(table[kept_row, r], room - 1)] = value


def combine_last(sent_row, kept_row, count_row, table, kept_in, received, sent, kept):
    def step(r, _):
        value = kept_in[r] + received[r].astype(F32)
        away = table[sent_row, r]

        @pl.when(away >= 0)
        def _():
            sent[jnp.minimum(away, sent.shape[0] - 1)] = value.astype(BF16)

        @pl.when(away < 0)
        def _():
            kept[jnp.minimum(table[kept_row, r], kept.shape[0] - 1)] = value

        return 0

    lax.fori_loop(0, jnp.minimum(table[count_row, 0], kept_in.shape[0]), step, 0)


def finish(count_row, place, table, *refs):
    ends, out = refs[:-1], refs[-1]
    count = table[count_row, 0]
    swapped = place[0] != 0
    for slot in range(out.shape[1]):
        mine = jnp.concatenate([end[slot] for end in ends[0::2]], axis=0)
        other = jnp.concatenate([end[slot] for end in ends[1::2]], axis=0).astype(F32)
        low, high = jnp.where(swapped, other, mine), jnp.where(swapped, mine, other)
        whole = jnp.concatenate([low, high], axis=0).T
        out[0, slot] = jnp.where(slot < count, whole, 0.0)


def axes_of(owner_count):
    bits = owner_count.bit_length() - 1
    if bits == 4:
        y, near, far = 1, 2, 3
        parts = ((1, (y, near, far)), (1, (near, y, far))), ((1, (y, far, near)), (1, (near, y, far)))
        turns = tuple((part, 0) for part in range(2)) + tuple((piece, n) for n in range(1, 4) for piece in range(4))
        return 0, (y, near), (far,), parts, turns
    pair, ends, rest = bits - 2, (0, bits - 1), tuple(range(1, bits - 2))
    parts = ((2, (*ends, *rest)),), ((2, (*ends[::-1], *rest)),)
    return pair, ends, rest, parts, tuple((piece, n) for n in range(bits) for piece in range(2))


def steps_of(axes):
    pair, _, _, parts, _ = axes
    steps = {}
    for part in parts:
        for _, order in part:
            order = (*order, pair)
            for n, bit in enumerate(order):
                steps[tuple(sorted(order[:n])), bit] = None
    return list(steps)


def rows_of(axes):
    names = ["order", "first", "last", "end", "fits"]
    names += [(step, kind) for step in steps_of(axes) for kind in ("sent", "kept")]
    return {name: n for n, name in enumerate(names)}


def make_plan(axes, usual, own_blocks, place, owners, columns, found, table):
    pair, rows = axes[0], rows_of(axes)
    count, places = owners.shape[1], columns.shape[1]
    me = place[2]
    across = lax.broadcasted_iota(jnp.int32, (count, count), 1)
    down = lax.broadcasted_iota(jnp.int32, (count, count), 0)
    owner_row, column_row = owners[...], columns[...]

    def as_column(row):
        size = row.shape[1]
        kept = jnp.where((across == down)[:size, :size], row.astype(F32), 0.0)
        return jnp.sum(kept, axis=1, keepdims=True).astype(jnp.int32)

    owner_col, column_col = as_column(owner_row), as_column(column_row)
    before = across < down
    differs_row, differs_col = owner_row ^ me, owner_col ^ me

    def alive(differs, done):
        return (differs & sum(1 << b for b in done)) == 0

    def number(mask):
        return jnp.where(mask, 1.0, 0.0)

    def rank(mask_row):
        return jnp.sum(jnp.where(before, number(mask_row), 0.0), axis=1, keepdims=True)

    def turned(column):
        return jnp.sum(jnp.where(across == down, column, 0.0), axis=0, keepdims=True)

    def write(name, row):
        table[pl.ds(rows[name], 1), :] = row.astype(jnp.int32)

    def going(done, bit):
        live, away = alive(differs_row, done), ((differs_row >> bit) & 1) == 1
        return rank(jnp.logical_and(live, away)), rank(jnp.logical_and(live, jnp.logical_not(away)))

    table[...] = jnp.zeros(table.shape, jnp.int32)
    table[pl.ds(rows["order"], 1), :] = (found[0:1, :] ^ me) * own_blocks + found[1:2, :]
    same = column_row == column_col
    place_at = lax.broadcasted_iota(jnp.int32, (places, places), 0).astype(F32)
    first = jnp.min(jnp.where(same, place_at, float(places)), axis=0, keepdims=True)
    table[pl.ds(rows["first"], 1), :places] = first.astype(jnp.int32)
    full, at_most, everything = float(count), None, ()
    for step in steps_of(axes):
        done, bit = step
        sent, kept = going(done, bit)
        if not done:
            write((step, "sent"), turned(sent))
            write((step, "kept"), turned(kept))
            continue
        live = rank(alive(differs_row, done))
        hit = jnp.logical_and(alive(differs_col, done), live == across.astype(F32))
        if bit == pair:
            sent, everything = jnp.where(((differs_col >> bit) & 1) == 1, sent, -1.0), done
        for kind, values in (("sent", sent), ("kept", kept)):
            write((step, kind), full + jnp.sum(jnp.where(hit, values - full, 0.0), axis=0, keepdims=True))
    for done, most in usual.items():
        mask = sum(1 << b for b in done)
        group = (owner_row & mask) == (owner_col & mask)
        over = jnp.max(jnp.sum(number(group), axis=1, keepdims=True), axis=0, keepdims=True) - most
        at_most = over if at_most is None else jnp.maximum(at_most, over)
    for name, done in (("last", everything), ("end", (*everything, pair))):
        total = jnp.sum(number(alive(differs_row, done)), axis=1, keepdims=True)
        write(name, jnp.broadcast_to(total, (1, count)))
    fits = jnp.zeros((1, 1), F32) if at_most is None else at_most
    write("fits", jnp.broadcast_to(number(fits <= 0.0), (1, count)))


def local(tokens, hidden_grad, masters, block_row, block_col, owners):
    owner_count = lax.axis_size("dp")
    me = lax.axis_index("dp")
    axes = axes_of(owner_count)
    pair, (bit_a, bit_b), rest, parts, turns = axes
    own_blocks, side = masters.shape[1], masters.shape[2]
    places, half, quarter = block_row.shape[1], side // 2, side // 8
    block_count = owners.shape[1]
    token_count = tokens.shape[0]
    capacity = 3 * block_count // owner_count
    place = jnp.stack([(me >> pair) & 1, lax.axis_index("tensor"), me]).astype(jnp.int32)
    place = jnp.concatenate([place, block_row[0], block_col[0]])

    def struct(shape, dtype):
        return jax.ShapeDtypeStruct(shape, dtype)

    with jax.named_scope("tokens"):
        shape = [struct((places, token_count, side), BF16)]
        near = call(functools.partial(select_rows, 0), "select_rows", shape, [SMEM, VMEM], [place, tokens[None]])[0]
        first_chosen, others = near, spread(tokens)[1:]
        if others:
            near = call(
                functools.partial(select_rows, 1), "select_rows", shape, [SMEM] + [VMEM] * (len(others) + 1),
                [place, *others, near],
            )[0]
        own_chosen = near
        masters, _ = lax.optimization_barrier((masters, first_chosen))

    with jax.named_scope("weights"):
        kept, sent = call(
            split_masters, "split_masters", [struct((own_blocks, half, side), BF16)] * 2, [SMEM, VMEM], [place, masters]
        )
        entries = [(0, b) for b in range(own_blocks)]

        def moved(found, bit):
            return [(delta ^ (1 << bit), b) for delta, b in found]

        got = swap(sent, "dp", pair)
        entries = entries + moved(entries, pair)
        later, got = lax.optimization_barrier((place, got))
        other_chosen = swap(own_chosen, "dp", pair)
        current = jnp.concatenate([kept, got], 0)
        for bit in rest[:0:-1]:
            current = jnp.concatenate([current, swap(current, "dp", bit)], 0)
            entries = entries + moved(entries, bit)
        far = swap(current, "dp", rest[0])
        heights = [sum(share for share, _ in part) * quarter for part in parts]
        own_up, *sent_up = call(
            split_upstream, "split_upstream",
            [struct((places, height, token_count), BF16) for height in (half, *heights)],
            [SMEM, pl.BlockSpec(memory_space=pltpu.HBM)], [later, hidden_grad], 0,
            [pltpu.VMEM((places, token_count, side), BF16), pltpu.SemaphoreType.DMA((places,))],
        )
        current, far, sent_up = lax.optimization_barrier((current, far, sent_up))
        near_a, near_b = swap(current, "dp", bit_a), swap(far, "dp", bit_b)
        entries_a, entries_b = entries + moved(entries, bit_a), moved(entries, rest[0])
        entries_b = entries_b + moved(entries_b, bit_b)
        found = entries_a + moved(entries_a, bit_b) + entries_b + moved(entries_b, bit_a)
        found = np.array(found, np.int32).T

    with jax.named_scope("plan"):

        def most_of(done):
            return min(block_count, (owner_count >> len(done)) * capacity)

        def load_of(done):
            return min(most_of(done), (block_count >> len(done)) + capacity)

        rows = rows_of(axes)
        settled = [tuple(sorted((*done, bit))) for done, bit in steps_of(axes)]
        usual = {done: load_of(done) for done in settled if load_of(done) < most_of(done)}
        table = call(
            functools.partial(make_plan, axes, usual, own_blocks), "make_plan",
            [struct((-(-len(rows) // 8) * 8, block_count), jnp.int32)], [SMEM] + [VMEM] * 3,
            [later, owners, block_col, jnp.asarray(found)],
        )[0]
        fits = table[rows["fits"], :1]
        for bit in range(lax.axis_size("tensor").bit_length() - 1):
            fits = jnp.minimum(fits, swap(fits, "tensor", bit))

    with jax.named_scope("weights"):
        near_a, near_b, table = lax.optimization_barrier((near_a, near_b, table))
        a0, b0 = jnp.concatenate([current, near_a], 0), jnp.concatenate([far, near_b], 0)
        a1, b1 = swap(a0, "dp", bit_b), swap(b0, "dp", bit_a)
        a1, b1, fits = lax.optimization_barrier((a1, b1, fits))

    with jax.named_scope("upstream"):
        other_up = [swap(sent, "dp", pair) for sent in sent_up]

    work = 2 * 2 * places * side * side * token_count
    with jax.named_scope("own_tokens"):
        weights, grad = call(
            functools.partial(own_part, rows), "own_part",
            [struct((places, side, side), BF16), struct((places, side, side), F32)], [SMEM] + [VMEM] * 6,
            [table, a0, a1, b0, b1, own_chosen, own_up], work, [pltpu.VMEM((places, side, token_count), F32)],
        )
    with jax.named_scope("other_tokens"):
        slope = call(
            functools.partial(other_slopes, rows), "other_slopes", [struct((places, side, token_count), F32)],
            [SMEM, VMEM, VMEM], [table, weights, other_chosen], work // 2,
            [pltpu.VMEM((places, side, token_count), F32)],
        )[0]

    def reduce(load, table, slope, other_chosen, other_up, grad):
        held, got, orders, firsts, start = [], [], [], [], 0
        for part in parts:
            firsts.append((len(orders), start))
            orders += [(*order, pair) for _, order in part]
            start += sum(share for share, _ in part) * quarter
        turn = None
        for at, n in turns:
            if n == 0:
                part, up, (piece, start) = parts[at], other_up[at], firsts[at]
                steps = [((), order[0]) for _, order in part]
                shapes = [(load(step[1:]) + 1, share * quarter, side) for step, (share, _) in zip(steps, part)]
                body, spec = functools.partial(other_part, rows, steps, start), [SMEM] + [VMEM] * 4
                args, scratch = [table, slope, other_chosen, up, grad], [pltpu.VMEM((places, 2 * up.shape[1], side), F32)]
            else:
                piece, order = at, orders[at]
                step = tuple(sorted(order[:n])), order[n]
                where = rows[step, "sent"], rows[step, "kept"]
                if order[n] == pair:
                    body, room = functools.partial(combine_last, *where, rows["last"]), capacity
                else:
                    body, room = functools.partial(combine, *where), load(order[: n + 1]) + 1
                shapes = [(room, *held[piece].shape[1:])]
                spec, args, scratch = [SMEM] + [VMEM] * 2, [table, held[piece], got[piece]], []
            if turn is not None:
                args[-1], _ = lax.optimization_barrier((args[-1], turn))
            outs = call(
                body, "combine" if n else "other_part", [struct(shape, dtype) for shape in shapes for dtype in (BF16, F32)],
                spec, args, 0 if n else work // 4, scratch,
            )
            turn = outs[1]
            if n == 0:
                held, got = held + [None] * len(part), got + [None] * len(part)
            for i, (sent, kept) in enumerate(zip(outs[0::2], outs[1::2])):
                held[piece + i], got[piece + i] = kept, swap(sent, "dp", orders[piece + i][n])
        return [end for both in zip(held, got) for end in both]

    operands = (table, slope, other_chosen, other_up, grad)
    ends = reduce(load_of, *operands)
    ends = lax.cond(fits[0] == 1, lambda ends, operands: ends, lambda ends, operands: reduce(most_of, *operands), ends, operands)
    return call(
        functools.partial(finish, rows["end"]), "finish", [struct((1, capacity, side, side), F32)],
        [SMEM, SMEM] + [VMEM] * len(ends), [place, table, *ends],
    )[0]


def solution(mesh):
    return jax.shard_map(
        local,
        mesh=mesh,
        in_specs=(
            P("dp", "tensor"),
            P("dp", "tensor"),
            P("tensor", "dp", None, None),
            P("tensor", None),
            P("tensor", None),
            P("tensor", None),
        ),
        out_specs=P("tensor", "dp", None, None),
        check_vma=False,
    )
```

```python
import functools

import jax
import jax.numpy as jnp
import numpy as np
from jax import lax
from jax.experimental import pallas as pl
from jax.experimental.pallas import tpu as pltpu
from jax.sharding import PartitionSpec as P

VMEM = pl.BlockSpec(memory_space=pltpu.VMEM)
SMEM = pl.BlockSpec(memory_space=pltpu.SMEM)
BF16 = jnp.bfloat16
F32 = jnp.float32


def call(body, name, outs, in_specs, args, flops=0, scratch=()):
    moved = sum(int(np.prod(o.shape)) * o.dtype.itemsize for o in outs)
    moved += sum(int(np.prod(a.shape)) * a.dtype.itemsize for a in args)
    return pl.pallas_call(
        body,
        name=name,
        out_shape=tuple(outs),
        in_specs=in_specs,
        out_specs=tuple(VMEM for _ in outs),
        scratch_shapes=list(scratch),
        compiler_params=pltpu.CompilerParams(vmem_limit_bytes=40 << 20),
        cost_estimate=pl.CostEstimate(flops=flops, bytes_accessed=moved, transcendentals=0),
    )(*args)


def swap(value, axis, bit):
    size = lax.axis_size(axis)
    return lax.ppermute(value, axis, [(i, i ^ (1 << bit)) for i in range(size)])


def spread(value):
    parts = [value[None]]
    for bit in range(lax.axis_size("tensor").bit_length() - 1):
        whole = parts[0] if len(parts) == 1 else jnp.concatenate(parts, 0)
        parts.append(swap(whole, "tensor", bit))
    return parts


def split_masters(masters, tokens, low, high):
    del tokens
    half = low.shape[1]
    for block in range(masters.shape[1]):
        turned = masters[0, block].T.astype(BF16)
        low[block], high[block] = turned[:half], turned[half:]


def split_upstream(place, grad, kept, *refs):
    parts, blocks, arrived = refs[:-2], refs[-2], refs[-1]
    count, half, side = kept.shape[0], kept.shape[1], kept.shape[2]

    def fetch(k):
        start = pl.multiple_of(place[3 + count + k] * side, side)
        return pltpu.make_async_copy(grad.at[:, pl.ds(start, side)], blocks.at[k], arrived.at[k])

    for k in range(count):
        fetch(k).start()
    for k in range(count):
        fetch(k).wait()
        turned = blocks[k].T
        low, high = turned[:half], turned[half:]
        swapped = place[0] != 0
        kept[k] = jnp.where(swapped, high, low)
        sent = jnp.where(swapped, low, high)
        start = 0
        for part in parts:
            part[k] = sent[start : start + part.shape[1]]
            start += part.shape[1]


def select_rows(first, place, *refs):
    sources, before, chosen = refs[:-1], None, refs[-1]
    side = chosen.shape[2]
    per_shard = sources[0].shape[2] // side
    for k in range(chosen.shape[0]):
        shard = place[3 + k] // per_shard
        start = pl.multiple_of((place[3 + k] - shard * per_shard) * side, side)
        offset = shard ^ place[1]
        value, at = None if first == 0 else before[k], first
        for source in sources:
            size = source.shape[0]
            here = source[jnp.clip(offset - at, 0, size - 1), :, pl.ds(start, side)]
            value = here if value is None else jnp.where(offset >= at, here, value)
            at += size
        chosen[k] = value


def add_duplicates(first, table, total):
    for k in range(1, total.shape[0]):

        @pl.when(table[first, k] != k)
        def _():
            total[table[first, k]] += total[k]


def slopes(gate, up):
    sigmoid = 0.5 + 0.5 * jnp.tanh(0.5 * gate)
    return sigmoid * up * (1.0 + gate * (1.0 - sigmoid)), sigmoid * gate


def project(weight, source):
    return lax.dot_general(weight, source, (((1,), (1,)), ((), ())), preferred_element_type=F32)


def term(upstream, gate_slope, up_slope, source):
    upstream = upstream.astype(F32)
    both = [(upstream * gate_slope).astype(BF16), (upstream * up_slope).astype(BF16)]
    return jnp.dot(jnp.concatenate(both, axis=0), source, preferred_element_type=F32)


def own_part(rows, table, *refs):
    sources, own_tokens, own_up, weights, grad, total = refs[:4], refs[4], refs[5], refs[6], refs[7], refs[8]
    places, half = own_up.shape[0], own_up.shape[1]
    position = 0
    for source in sources:
        for p in range(source.shape[0]):
            block = table[rows["order"], position + p]
            up = (block >= places).astype(jnp.int32)
            weights[block - up * places, pl.ds(pl.multiple_of(up * half, half), half), :] = source[p]
        position += source.shape[0]
    for k in range(places):
        total[k] = project(weights[k], own_tokens[k])
    add_duplicates(rows["first"], table, total)
    for k in range(places):
        first = table[rows["first"], k]
        grad[k] = term(own_up[k], *slopes(total[first, :half], total[first, half:]), own_tokens[k])


def other_slopes(rows, table, weights, other_tokens, slope, total):
    places, half = weights.shape[0], weights.shape[1] // 2
    for k in range(places):
        total[k] = project(weights[k], other_tokens[k])
    add_duplicates(rows["first"], table, total)
    for k in range(places):
        first = table[rows["first"], k]
        slope[k, :half], slope[k, half:] = slopes(total[first, :half], total[first, half:])


def scalar(table, row):
    return jnp.max(table[pl.ds(row, 1), :].astype(F32)).astype(jnp.int32)


def other_part(rows, steps, start, table, slope, other_tokens, other_up, grad, *refs):
    outs, total, ordered = refs[: 2 * len(steps)], refs[2 * len(steps)], refs[2 * len(steps) + 1 :]
    places, height, half = other_up.shape[0], other_up.shape[1], grad.shape[1] // 2
    gate, up = pl.ds(start, height), pl.ds(half + start, height)
    for k in range(places):
        result = term(other_up[k], slope[k, gate], slope[k, up], other_tokens[k])
        total[k, :height] = grad[k, gate] + result[:height]
        total[k, height:] = grad[k, up] + result[height:]
    first = 0
    for n, (order, step) in enumerate(steps):
        sent, kept = outs[2 * n], outs[2 * n + 1]
        room, size = sent.shape[0], sent.shape[1]
        for block in range(2 * places):
            which, k = divmod(block, places)
            ordered[n][table[rows[order, "at"], block]] = total[k, pl.ds(which * height + first, size), :]
        sent[...] = ordered[n][pl.ds(table[rows[step, "sent"], 0], room)].astype(BF16)
        kept[...] = ordered[n][pl.ds(table[rows[step, "kept"], 0], room)]
        first += size


def combine(sent_row, kept_row, pieces, table, *refs):
    kept_in, received, (sent, kept, total) = refs[:pieces], refs[pieces : 2 * pieces], refs[2 * pieces :]
    count, room, start = kept_in[0].shape[0], sent.shape[0], 0
    for mine, other in zip(kept_in, received):
        total[:count, start : start + mine.shape[1]] = mine[...] + other[...].astype(F32)
        start += mine.shape[1]
    sent[...] = total[pl.ds(jnp.minimum(scalar(table, sent_row), count), room)].astype(BF16)
    kept[...] = total[pl.ds(jnp.minimum(scalar(table, kept_row), count), room)]


def finish(count_row, pair_row, table, *refs):
    ends, out = refs[:-1], refs[-1]
    count, swapped = scalar(table, count_row), scalar(table, pair_row) != 0
    for slot in range(out.shape[1]):
        mine = jnp.concatenate([end[slot] for end in ends[0::2]], axis=0)
        other = jnp.concatenate([end[slot] for end in ends[1::2]], axis=0).astype(F32)
        low, high = jnp.where(swapped, other, mine), jnp.where(swapped, mine, other)
        whole = jnp.concatenate([low, high], axis=0).T
        out[0, slot] = jnp.where(slot < count, whole, 0.0)


def axes_of(owner_count):
    bits = owner_count.bit_length() - 1
    if bits == 4:
        y, near, far = 1, 2, 3
        parts = ((1, (near, y, far)), (1, (y, far, near))), ((1, (y, near, far)), (1, (near, far, y)))
        turns = tuple(((part,), 0) for part in range(2)) + tuple(((piece,), n) for n in range(1, 4) for piece in range(4))
        return 0, (y, near), (far,), parts, turns
    pair, ends, rest = bits - 2, (0, bits - 1), tuple(range(1, bits - 2))
    parts = ((2, (*ends, *rest)),), ((2, (*ends[::-1], *rest)),)
    return pair, ends, rest, parts, tuple(((piece,), n) for n in range(bits) for piece in range(2))


def orders_of(axes):
    return list(dict.fromkeys((*order, axes[0]) for part in axes[3] for _, order in part))


def steps_of(axes):
    return list(dict.fromkeys((tuple(sorted(o[:n])), bit) for o in orders_of(axes) for n, bit in enumerate(o)))


def rows_of(axes):
    names = ["order", "first", "end", "pair", "fits"]
    names += [(order, "at") for order in orders_of(axes)]
    names += [(step, kind) for step in steps_of(axes) for kind in ("sent", "kept")]
    return {name: n for n, name in enumerate(names)}


def make_plan(axes, usual, own_blocks, place, owners, columns, found, table):
    pair, rows = axes[0], rows_of(axes)
    count, places = owners.shape[1], columns.shape[1]
    me = place[2]
    across = lax.broadcasted_iota(jnp.int32, (count, count), 1)
    down = lax.broadcasted_iota(jnp.int32, (count, count), 0)
    owner_row, column_row = owners[...], columns[...]

    def as_column(row):
        size = row.shape[1]
        kept = jnp.where((across == down)[:size, :size], row.astype(F32), 0.0)
        return jnp.sum(kept, axis=1, keepdims=True).astype(jnp.int32)

    def number(mask):
        return jnp.where(mask, 1.0, 0.0)

    def write(name, row):
        table[pl.ds(rows[name], 1), :] = jnp.broadcast_to(row, (1, count)).astype(jnp.int32)

    owner_col, column_col = as_column(owner_row), as_column(column_row)
    table[...] = jnp.zeros(table.shape, jnp.int32)
    write("order", (found[0:1, :] ^ me) * own_blocks + found[1:2, :])
    same = column_row == column_col
    place_at = lax.broadcasted_iota(jnp.int32, (places, places), 0).astype(F32)
    first = jnp.min(jnp.where(same, place_at, float(places)), axis=0, keepdims=True)
    table[pl.ds(rows["first"], 1), :places] = first.astype(jnp.int32)
    write("pair", jnp.full((1, 1), (me >> pair) & 1, jnp.int32))
    for order in orders_of(axes):

        def key(owner):
            return sum(((owner >> bit) & 1) << n for n, bit in enumerate(order[::-1]))

        ahead = key(owner_col) < key(owner_row)
        ahead = jnp.logical_or(ahead, jnp.logical_and(key(owner_col) == key(owner_row), down < across))
        write((order, "at"), jnp.sum(number(ahead), axis=0, keepdims=True))

    def alive(done):
        return ((owner_row ^ me) & sum(1 << b for b in done)) == 0

    for step in steps_of(axes):
        done, bit = step
        low = jnp.logical_and(alive(done), ((owner_row >> bit) & 1) == 0)
        total, mine = jnp.sum(number(low), axis=1, keepdims=True), ((me >> bit) & 1).astype(F32)
        write((step, "sent"), total * (1.0 - mine))
        write((step, "kept"), total * mine)
    everything = alive((*axes[1], *axes[2], pair))
    write("end", jnp.sum(number(everything), axis=1, keepdims=True))
    over = jnp.zeros((1, 1), F32)
    for done, most in usual.items():
        mask = sum(1 << b for b in done)
        group = (owner_row & mask) == (owner_col & mask)
        taken = jnp.max(jnp.sum(number(group), axis=1, keepdims=True), axis=0, keepdims=True)
        over = jnp.maximum(over, taken - most)
    write("fits", number(over <= 0.0))


def local(tokens, hidden_grad, masters, block_row, block_col, owners):
    owner_count = lax.axis_size("dp")
    me = lax.axis_index("dp")
    axes = axes_of(owner_count)
    pair, (bit_a, bit_b), rest, parts, turns = axes
    own_blocks, side = masters.shape[1], masters.shape[2]
    places, half, quarter = block_row.shape[1], side // 2, side // 8
    block_count = owners.shape[1]
    token_count = tokens.shape[0]
    capacity = 3 * block_count // owner_count
    place = jnp.stack([(me >> pair) & 1, lax.axis_index("tensor"), me]).astype(jnp.int32)
    place = jnp.concatenate([place, block_row[0], block_col[0]])

    def struct(shape, dtype):
        return jax.ShapeDtypeStruct(shape, dtype)

    with jax.named_scope("tokens"):
        own_chosen = call(
            functools.partial(select_rows, 0), "select_rows", [struct((places, token_count, side), BF16)],
            [SMEM] + [VMEM] * lax.axis_size("tensor").bit_length(), [place, *spread(tokens)],
        )[0]

    with jax.named_scope("weights"):
        low, high = call(
            split_masters, "split_masters", [struct((own_blocks, half, side), BF16)] * 2, [VMEM] * 2, [masters, tokens]
        )
        upper = ((me >> pair) & 1) == 1
        kept, sent = jnp.where(upper, high, low), jnp.where(upper, low, high)
        entries = [(0, b) for b in range(own_blocks)]

        def moved(found, bit):
            return [(delta ^ (1 << bit), b) for delta, b in found]

        got = swap(sent, "dp", pair)
        entries = entries + moved(entries, pair)
        later, got = lax.optimization_barrier((place, got))
        other_chosen = swap(own_chosen, "dp", pair)
        current = jnp.concatenate([kept, got], 0)
        for bit in rest[:0:-1]:
            current = jnp.concatenate([current, swap(current, "dp", bit)], 0)
            entries = entries + moved(entries, bit)
        far = swap(current, "dp", rest[0])
        heights = [sum(share for share, _ in part) * quarter for part in parts]
        own_up, *sent_up = call(
            split_upstream, "split_upstream",
            [struct((places, height, token_count), BF16) for height in (half, *heights)],
            [SMEM, pl.BlockSpec(memory_space=pltpu.HBM)], [later, hidden_grad], 0,
            [pltpu.VMEM((places, token_count, side), BF16), pltpu.SemaphoreType.DMA((places,))],
        )
        current, far, sent_up = lax.optimization_barrier((current, far, sent_up))
        near_a, near_b = swap(current, "dp", bit_a), swap(far, "dp", bit_b)
        entries_a, entries_b = entries + moved(entries, bit_a), moved(entries, rest[0])
        entries_b = entries_b + moved(entries_b, bit_b)
        found = entries_a + moved(entries_a, bit_b) + entries_b + moved(entries_b, bit_a)
        found = np.array(found, np.int32).T

    with jax.named_scope("plan"):

        def most_of(done):
            return min(block_count, (owner_count >> len(done)) * capacity)

        def load_of(done):
            return min(most_of(done), (block_count >> len(done)) + capacity)

        rows = rows_of(axes)
        settled = [tuple(sorted((*done, bit))) for done, bit in steps_of(axes)]
        usual = {done: load_of(done) for done in settled if load_of(done) < most_of(done)}
        table = call(
            functools.partial(make_plan, axes, usual, own_blocks), "make_plan",
            [struct((-(-len(rows) // 8) * 8, block_count), jnp.int32)], [SMEM] + [VMEM] * 3,
            [later, owners, block_col, jnp.asarray(found)],
        )[0]
        fits = table[rows["fits"], :1]
        for bit in range(lax.axis_size("tensor").bit_length() - 1):
            fits = jnp.minimum(fits, swap(fits, "tensor", bit))

    with jax.named_scope("weights"):
        near_a, near_b, table = lax.optimization_barrier((near_a, near_b, table))
        a0, b0 = jnp.concatenate([current, near_a], 0), jnp.concatenate([far, near_b], 0)
        a1, b1 = swap(a0, "dp", bit_b), swap(b0, "dp", bit_a)
        a1, b1, fits = lax.optimization_barrier((a1, b1, fits))

    with jax.named_scope("upstream"):
        other_up = [swap(sent, "dp", pair) for sent in sent_up]

    work = 2 * 2 * places * side * side * token_count
    with jax.named_scope("own_tokens"):
        weights, grad = call(
            functools.partial(own_part, rows), "own_part",
            [struct((places, side, side), BF16), struct((places, side, side), F32)], [SMEM] + [VMEM] * 6,
            [table, a0, a1, b0, b1, own_chosen, own_up], work, [pltpu.VMEM((places, side, token_count), F32)],
        )
    with jax.named_scope("other_tokens"):
        slope = call(
            functools.partial(other_slopes, rows), "other_slopes", [struct((places, side, token_count), F32)],
            [SMEM, VMEM, VMEM], [table, weights, other_chosen], work // 2,
            [pltpu.VMEM((places, side, token_count), F32)],
        )[0]

    def reduce(load, table, slope, other_chosen, other_up, grad):
        orders, firsts, start = [], [], 0
        for part in parts:
            firsts.append((len(orders), start))
            orders += [(*order, pair) for _, order in part]
            start += sum(share for share, _ in part) * quarter
        state, turn = {}, None
        for group, n in turns:
            order = orders[group[0]]
            if n == 0:
                (at,) = group
                part, up, (piece, start) = parts[at], other_up[at], firsts[at]
                steps = [((*order, pair), ((), order[0])) for _, order in part]
                shapes = [(load(order[:1]), share * quarter, side) for share, order in part]
                body, spec = functools.partial(other_part, rows, steps, start), [SMEM] + [VMEM] * 4
                args, scratch = [table, slope, other_chosen, up, grad], [pltpu.VMEM((places, 2 * up.shape[1], side), F32)]
                scratch += [pltpu.VMEM((block_count + room, *rest_of), F32) for room, *rest_of in shapes]
                made = [(piece + i,) for i in range(len(part))]
            else:
                joined = [state.pop(key) for key in sorted(state) if set(key) <= set(group)]
                step = tuple(sorted(order[:n])), order[n]
                body = functools.partial(combine, rows[step, "sent"], rows[step, "kept"], len(joined))
                room, was, height = load(order[: n + 1]), joined[0][0].shape[0], sum(k.shape[1] for k, _ in joined)
                shapes, spec = [(room, height, side)], [VMEM] * (1 + 2 * len(joined))
                args = [table, *(k for k, _ in joined), *(g for _, g in joined)]
                scratch, made = [pltpu.VMEM((was + room, height, side), F32)], [group]
            if turn is not None:
                args[-1], _ = lax.optimization_barrier((args[-1], turn))
            outs = call(
                body, "combine" if n else "other_part", [struct(shape, dtype) for shape in shapes for dtype in (BF16, F32)],
                spec, args, 0 if n else work // 4, scratch,
            )
            turn = outs[1]
            for key, sent, kept in zip(made, outs[0::2], outs[1::2]):
                state[key] = kept, swap(sent, "dp", orders[key[0]][n])
        return [end for key in sorted(state) for end in state[key]]

    operands = (table, slope, other_chosen, other_up, grad)
    ends = reduce(load_of, *operands)
    ends = lax.cond(fits[0] == 1, lambda ends, operands: ends, lambda ends, operands: reduce(most_of, *operands), ends, operands)
    return call(
        functools.partial(finish, rows["end"], rows["pair"]), "finish", [struct((1, capacity, side, side), F32)],
        [VMEM] * (1 + len(ends)), [table, *ends],
    )[0]


def solution(mesh):
    return jax.shard_map(
        local,
        mesh=mesh,
        in_specs=(
            P("dp", "tensor"),
            P("dp", "tensor"),
            P("tensor", "dp", None, None),
            P("tensor", None),
            P("tensor", None),
            P("tensor", None),
        ),
        out_specs=P("tensor", "dp", None, None),
        check_vma=False,
    )
```

```python
import functools

import jax
import jax.numpy as jnp
import numpy as np
from jax import lax
from jax.experimental import pallas as pl
from jax.experimental.pallas import tpu as pltpu
from jax.sharding import PartitionSpec as P

VMEM = pl.BlockSpec(memory_space=pltpu.VMEM)
SMEM = pl.BlockSpec(memory_space=pltpu.SMEM)
BF16 = jnp.bfloat16
F32 = jnp.float32


def call(body, name, outs, in_specs, args, flops=0, scratch=()):
    moved = sum(int(np.prod(o.shape)) * o.dtype.itemsize for o in outs)
    moved += sum(int(np.prod(a.shape)) * a.dtype.itemsize for a in args)
    return pl.pallas_call(
        body,
        name=name,
        out_shape=tuple(outs),
        in_specs=in_specs,
        out_specs=tuple(VMEM for _ in outs),
        scratch_shapes=list(scratch),
        compiler_params=pltpu.CompilerParams(vmem_limit_bytes=40 << 20),
        cost_estimate=pl.CostEstimate(flops=flops, bytes_accessed=moved, transcendentals=0),
    )(*args)


def swap(value, axis, bit):
    size = lax.axis_size(axis)
    return lax.ppermute(value, axis, [(i, i ^ (1 << bit)) for i in range(size)])


def spread(value):
    parts = [value[None]]
    for bit in range(lax.axis_size("tensor").bit_length() - 1):
        whole = parts[0] if len(parts) == 1 else jnp.concatenate(parts, 0)
        parts.append(swap(whole, "tensor", bit))
    return parts


def split_masters(masters, tokens, low, high):
    del tokens
    half = low.shape[1]
    for block in range(masters.shape[1]):
        turned = masters[0, block].T.astype(BF16)
        low[block], high[block] = turned[:half], turned[half:]


def split_upstream(place, grad, kept, *refs):
    parts, blocks, arrived = refs[:-2], refs[-2], refs[-1]
    count, half, side = kept.shape[0], kept.shape[1], kept.shape[2]

    def fetch(k):
        start = pl.multiple_of(place[3 + count + k] * side, side)
        return pltpu.make_async_copy(grad.at[:, pl.ds(start, side)], blocks.at[k], arrived.at[k])

    for k in range(count):
        fetch(k).start()
    for k in range(count):
        fetch(k).wait()
        turned = blocks[k].T
        low, high = turned[:half], turned[half:]
        swapped = place[0] != 0
        kept[k] = jnp.where(swapped, high, low)
        sent = jnp.where(swapped, low, high)
        start = 0
        for part in parts:
            part[k] = sent[start : start + part.shape[1]]
            start += part.shape[1]


def select_rows(first, place, *refs):
    sources, before, chosen = refs[:-1], None, refs[-1]
    side = chosen.shape[2]
    per_shard = sources[0].shape[2] // side
    for k in range(chosen.shape[0]):
        shard = place[3 + k] // per_shard
        start = pl.multiple_of((place[3 + k] - shard * per_shard) * side, side)
        offset = shard ^ place[1]
        value, at = None if first == 0 else before[k], first
        for source in sources:
            size = source.shape[0]
            here = source[jnp.clip(offset - at, 0, size - 1), :, pl.ds(start, side)]
            value = here if value is None else jnp.where(offset >= at, here, value)
            at += size
        chosen[k] = value


def add_duplicates(first, table, total):
    for k in range(1, total.shape[0]):

        @pl.when(table[first, k] != k)
        def _():
            total[table[first, k]] += total[k]


def slopes(gate, up):
    sigmoid = 0.5 + 0.5 * jnp.tanh(0.5 * gate)
    return sigmoid * up * (1.0 + gate * (1.0 - sigmoid)), sigmoid * gate


def project(weight, source):
    return lax.dot_general(weight, source, (((1,), (1,)), ((), ())), preferred_element_type=F32)


def term(upstream, gate_slope, up_slope, source):
    upstream = upstream.astype(F32)
    both = [(upstream * gate_slope).astype(BF16), (upstream * up_slope).astype(BF16)]
    return jnp.dot(jnp.concatenate(both, axis=0), source, preferred_element_type=F32)


def own_part(rows, table, *refs):
    sources, own_tokens, own_up, weights, grad, total = refs[:4], refs[4], refs[5], refs[6], refs[7], refs[8]
    places, half = own_up.shape[0], own_up.shape[1]
    position = 0
    for source in sources:
        for p in range(source.shape[0]):
            block = table[rows["order"], position + p]
            up = (block >= places).astype(jnp.int32)
            weights[block - up * places, pl.ds(pl.multiple_of(up * half, half), half), :] = source[p]
        position += source.shape[0]
    for k in range(places):
        total[k] = project(weights[k], own_tokens[k])
    add_duplicates(rows["first"], table, total)
    for k in range(places):
        first = table[rows["first"], k]
        grad[k] = term(own_up[k], *slopes(total[first, :half], total[first, half:]), own_tokens[k])


def other_slopes(rows, table, weights, other_tokens, slope, total):
    places, half = weights.shape[0], weights.shape[1] // 2
    for k in range(places):
        total[k] = project(weights[k], other_tokens[k])
    add_duplicates(rows["first"], table, total)
    for k in range(places):
        first = table[rows["first"], k]
        slope[k, :half], slope[k, half:] = slopes(total[first, :half], total[first, half:])


def scalar(table, row):
    return jnp.max(table[pl.ds(row, 1), :].astype(F32)).astype(jnp.int32)


def other_part(rows, steps, start, plan, slope, other_tokens, other_up, grad, *refs):
    outs, (table, arrived, total, *ordered) = refs[: 2 * len(steps)], refs[2 * len(steps) :]
    copy = pltpu.make_async_copy(plan, table, arrived)
    copy.start()
    places, height, half = other_up.shape[0], other_up.shape[1], grad.shape[1] // 2
    gate, up = pl.ds(start, height), pl.ds(half + start, height)
    for k in range(places):
        result = term(other_up[k], slope[k, gate], slope[k, up], other_tokens[k])
        total[k, :height] = grad[k, gate] + result[:height]
        total[k, height:] = grad[k, up] + result[height:]
    copy.wait()
    first = 0
    for n, (order, step) in enumerate(steps):
        sent, kept = outs[2 * n], outs[2 * n + 1]
        room, size = sent.shape[0], sent.shape[1]
        for block in range(2 * places):
            which, k = divmod(block, places)
            ordered[n][table[rows[order, "at"], block]] = total[k, pl.ds(which * height + first, size), :]
        sent[...] = ordered[n][pl.ds(table[rows[step, "sent"], 0], room)].astype(BF16)
        kept[...] = ordered[n][pl.ds(table[rows[step, "kept"], 0], room)]
        first += size


def combine(sent_row, kept_row, pieces, table, *refs):
    kept_in, received, (sent, kept, total) = refs[:pieces], refs[pieces : 2 * pieces], refs[2 * pieces :]
    count, room, start = kept_in[0].shape[0], sent.shape[0], 0
    for mine, other in zip(kept_in, received):
        total[:count, start : start + mine.shape[1]] = mine[...] + other[...].astype(F32)
        start += mine.shape[1]
    sent[...] = total[pl.ds(jnp.minimum(scalar(table, sent_row), count), room)].astype(BF16)
    kept[...] = total[pl.ds(jnp.minimum(scalar(table, kept_row), count), room)]


def finish(count_row, pair_row, table, *refs):
    ends, out = refs[:-1], refs[-1]
    count, swapped = scalar(table, count_row), scalar(table, pair_row) != 0
    for slot in range(out.shape[1]):
        mine = jnp.concatenate([end[slot] for end in ends[0::2]], axis=0)
        other = jnp.concatenate([end[slot] for end in ends[1::2]], axis=0).astype(F32)
        low, high = jnp.where(swapped, other, mine), jnp.where(swapped, mine, other)
        whole = jnp.concatenate([low, high], axis=0).T
        out[0, slot] = jnp.where(slot < count, whole, 0.0)


def axes_of(owner_count):
    bits = owner_count.bit_length() - 1
    if bits == 4:
        y, near, far = 1, 2, 3
        parts = ((1, (near, y, far)), (1, (y, far, near))), ((1, (near, y, far)), (1, (y, near, far)))
        turns = tuple(((part,), 0) for part in range(2)) + tuple(((piece,), n) for n in range(1, 4) for piece in range(4))
        return 0, (y, near), (far,), parts, turns
    pair, ends, rest = bits - 2, (0, bits - 1), tuple(range(1, bits - 2))
    parts = ((2, (*ends, *rest)),), ((2, (*ends[::-1], *rest)),)
    return pair, ends, rest, parts, tuple(((piece,), n) for n in range(bits) for piece in range(2))


def orders_of(axes):
    return list(dict.fromkeys((*order, axes[0]) for part in axes[3] for _, order in part))


def steps_of(axes):
    return list(dict.fromkeys((tuple(sorted(o[:n])), bit) for o in orders_of(axes) for n, bit in enumerate(o)))


def rows_of(axes):
    names = ["order", "first", "end", "pair", "fits"]
    names += [(order, "at") for order in orders_of(axes)]
    names += [(step, kind) for step in steps_of(axes) for kind in ("sent", "kept")]
    return {name: n for n, name in enumerate(names)}


def make_plan(axes, usual, own_blocks, place, columns, found, *refs):
    pair, rows, owners, table = axes[0], rows_of(axes), refs[:-1], refs[-1]
    count, places = owners[0].shape[1], columns.shape[1]
    me = place[2]
    across = lax.broadcasted_iota(jnp.int32, (count, count), 1)
    down = lax.broadcasted_iota(jnp.int32, (count, count), 0)
    owner_row, column_row = owners[0][...], columns[...]

    def as_column(row):
        size = row.shape[1]
        kept = jnp.where((across == down)[:size, :size], row.astype(F32), 0.0)
        return jnp.sum(kept, axis=1, keepdims=True).astype(jnp.int32)

    def number(mask):
        return jnp.where(mask, 1.0, 0.0)

    def write(name, row):
        table[pl.ds(rows[name], 1), :] = jnp.broadcast_to(row, (1, count)).astype(jnp.int32)

    owner_col, column_col = as_column(owner_row), as_column(column_row)
    table[...] = jnp.zeros(table.shape, jnp.int32)
    write("order", (found[0:1, :] ^ me) * own_blocks + found[1:2, :])
    same = column_row == column_col
    place_at = lax.broadcasted_iota(jnp.int32, (places, places), 0).astype(F32)
    first = jnp.min(jnp.where(same, place_at, float(places)), axis=0, keepdims=True)
    table[pl.ds(rows["first"], 1), :places] = first.astype(jnp.int32)
    write("pair", jnp.full((1, 1), (me >> pair) & 1, jnp.int32))
    for order in orders_of(axes):

        def key(owner):
            return sum(((owner >> bit) & 1) << n for n, bit in enumerate(order[::-1]))

        ahead = key(owner_col) < key(owner_row)
        ahead = jnp.logical_or(ahead, jnp.logical_and(key(owner_col) == key(owner_row), down < across))
        write((order, "at"), jnp.sum(number(ahead), axis=0, keepdims=True))

    def alive(done):
        return ((owner_row ^ me) & sum(1 << b for b in done)) == 0

    for step in steps_of(axes):
        done, bit = step
        low = jnp.logical_and(alive(done), ((owner_row >> bit) & 1) == 0)
        total, mine = jnp.sum(number(low), axis=1, keepdims=True), ((me >> bit) & 1).astype(F32)
        write((step, "sent"), total * (1.0 - mine))
        write((step, "kept"), total * mine)
    everything = alive((*axes[1], *axes[2], pair))
    write("end", jnp.sum(number(everything), axis=1, keepdims=True))
    over = jnp.zeros((1, 1), F32)
    for row in [part[n : n + 1, :] for part in owners for n in range(part.shape[0])]:
        column = as_column(row)
        for done, most in usual.items():
            mask = sum(1 << b for b in done)
            group = (row & mask) == (column & mask)
            taken = jnp.max(jnp.sum(number(group), axis=1, keepdims=True), axis=0, keepdims=True)
            over = jnp.maximum(over, taken - most)
    write("fits", number(over <= 0.0))


def local(tokens, hidden_grad, masters, block_row, block_col, owners):
    owner_count = lax.axis_size("dp")
    me = lax.axis_index("dp")
    axes = axes_of(owner_count)
    pair, (bit_a, bit_b), rest, parts, turns = axes
    own_blocks, side = masters.shape[1], masters.shape[2]
    places, half, quarter = block_row.shape[1], side // 2, side // 8
    block_count = owners.shape[1]
    token_count = tokens.shape[0]
    capacity = 3 * block_count // owner_count
    place = jnp.stack([(me >> pair) & 1, lax.axis_index("tensor"), me]).astype(jnp.int32)
    place = jnp.concatenate([place, block_row[0], block_col[0]])

    def struct(shape, dtype):
        return jax.ShapeDtypeStruct(shape, dtype)

    with jax.named_scope("tokens"):
        all_owners = [part.reshape(-1, block_count) for part in spread(owners)]
        own_chosen = call(
            functools.partial(select_rows, 0), "select_rows", [struct((places, token_count, side), BF16)],
            [SMEM] + [VMEM] * lax.axis_size("tensor").bit_length(), [place, *spread(tokens)],
        )[0]

    with jax.named_scope("weights"):
        low, high = call(
            split_masters, "split_masters", [struct((own_blocks, half, side), BF16)] * 2, [VMEM] * 2, [masters, tokens]
        )
        upper = ((me >> pair) & 1) == 1
        kept, sent = jnp.where(upper, high, low), jnp.where(upper, low, high)
        entries = [(0, b) for b in range(own_blocks)]

        def moved(found, bit):
            return [(delta ^ (1 << bit), b) for delta, b in found]

        got = swap(sent, "dp", pair)
        entries = entries + moved(entries, pair)
        later, got = lax.optimization_barrier((place, got))
        other_chosen = swap(own_chosen, "dp", pair)
        current = jnp.concatenate([kept, got], 0)
        for bit in rest[:0:-1]:
            current = jnp.concatenate([current, swap(current, "dp", bit)], 0)
            entries = entries + moved(entries, bit)
        far = swap(current, "dp", rest[0])
        heights = [sum(share for share, _ in part) * quarter for part in parts]
        own_up, *sent_up = call(
            split_upstream, "split_upstream",
            [struct((places, height, token_count), BF16) for height in (half, *heights)],
            [SMEM, pl.BlockSpec(memory_space=pltpu.HBM)], [later, hidden_grad], 0,
            [pltpu.VMEM((places, token_count, side), BF16), pltpu.SemaphoreType.DMA((places,))],
        )
        current, far, sent_up = lax.optimization_barrier((current, far, sent_up))
        near_a, near_b = swap(current, "dp", bit_a), swap(far, "dp", bit_b)
        entries_a, entries_b = entries + moved(entries, bit_a), moved(entries, rest[0])
        entries_b = entries_b + moved(entries_b, bit_b)
        found = entries_a + moved(entries_a, bit_b) + entries_b + moved(entries_b, bit_a)
        found = np.array(found, np.int32).T

    with jax.named_scope("plan"):

        def most_of(done):
            return min(block_count, (owner_count >> len(done)) * capacity)

        def load_of(done):
            return min(most_of(done), (block_count >> len(done)) + capacity)

        rows = rows_of(axes)
        settled = [tuple(sorted((*done, bit))) for done, bit in steps_of(axes)]
        usual = {done: load_of(done) for done in settled if load_of(done) < most_of(done)}
        table = call(
            functools.partial(make_plan, axes, usual, own_blocks), "make_plan",
            [struct((-(-len(rows) // 8) * 8, block_count), jnp.int32)], [SMEM] + [VMEM] * (2 + len(all_owners)),
            [later, block_col, jnp.asarray(found), *all_owners],
        )[0]

    with jax.named_scope("weights"):
        near_a, near_b, table = lax.optimization_barrier((near_a, near_b, table))
        a0, b0 = jnp.concatenate([current, near_a], 0), jnp.concatenate([far, near_b], 0)
        a1, b1 = swap(a0, "dp", bit_b), swap(b0, "dp", bit_a)

    with jax.named_scope("upstream"):
        other_up = [swap(sent, "dp", pair) for sent in sent_up]

    work = 2 * 2 * places * side * side * token_count
    with jax.named_scope("own_tokens"):
        weights, grad = call(
            functools.partial(own_part, rows), "own_part",
            [struct((places, side, side), BF16), struct((places, side, side), F32)], [SMEM] + [VMEM] * 6,
            [table, a0, a1, b0, b1, own_chosen, own_up], work, [pltpu.VMEM((places, side, token_count), F32)],
        )
    with jax.named_scope("other_tokens"):
        slope = call(
            functools.partial(other_slopes, rows), "other_slopes", [struct((places, side, token_count), F32)],
            [SMEM, VMEM, VMEM], [table, weights, other_chosen], work // 2,
            [pltpu.VMEM((places, side, token_count), F32)],
        )[0]

    def reduce(load, table, slope, other_chosen, other_up, grad):
        orders, firsts, start = [], [], 0
        for part in parts:
            firsts.append((len(orders), start))
            orders += [(*order, pair) for _, order in part]
            start += sum(share for share, _ in part) * quarter
        state, turn = {}, None
        for group, n in turns:
            order = orders[group[0]]
            if n == 0:
                (at,) = group
                part, up, (piece, start) = parts[at], other_up[at], firsts[at]
                steps = [((*order, pair), ((), order[0])) for _, order in part]
                shapes = [(load(order[:1]), share * quarter, side) for share, order in part]
                body, spec = functools.partial(other_part, rows, steps, start), [VMEM] * 5
                args = [table, slope, other_chosen, up, grad]
                scratch = [pltpu.SMEM(table.shape, jnp.int32), pltpu.SemaphoreType.DMA]
                scratch += [pltpu.VMEM((places, 2 * up.shape[1], side), F32)]
                scratch += [pltpu.VMEM((block_count + room, *rest_of), F32) for room, *rest_of in shapes]
                made = [(piece + i,) for i in range(len(part))]
            else:
                joined = [state.pop(key) for key in sorted(state) if set(key) <= set(group)]
                step = tuple(sorted(order[:n])), order[n]
                body = functools.partial(combine, rows[step, "sent"], rows[step, "kept"], len(joined))
                room, was, height = load(order[: n + 1]), joined[0][0].shape[0], sum(k.shape[1] for k, _ in joined)
                shapes, spec = [(room, height, side)], [VMEM] * (1 + 2 * len(joined))
                args = [table, *(k for k, _ in joined), *(g for _, g in joined)]
                scratch, made = [pltpu.VMEM((was + room, height, side), F32)], [group]
            if turn is not None:
                args[-1], _ = lax.optimization_barrier((args[-1], turn))
            outs = call(
                body, "combine" if n else "other_part", [struct(shape, dtype) for shape in shapes for dtype in (BF16, F32)],
                spec, args, 0 if n else work // 4, scratch,
            )
            turn = outs[1]
            for key, sent, kept in zip(made, outs[0::2], outs[1::2]):
                state[key] = kept, swap(sent, "dp", orders[key[0]][n])
        return [end for key in sorted(state) for end in state[key]]

    operands = (table, slope, other_chosen, other_up, grad)
    ends = reduce(load_of, *operands)
    ends = lax.cond(table[rows["fits"], 0] == 1, lambda ends, operands: ends, lambda ends, operands: reduce(most_of, *operands), ends, operands)
    return call(
        functools.partial(finish, rows["end"], rows["pair"]), "finish", [struct((1, capacity, side, side), F32)],
        [VMEM] * (1 + len(ends)), [table, *ends],
    )[0]


def solution(mesh):
    return jax.shard_map(
        local,
        mesh=mesh,
        in_specs=(
            P("dp", "tensor"),
            P("dp", "tensor"),
            P("tensor", "dp", None, None),
            P("tensor", None),
            P("tensor", None),
            P("tensor", None),
        ),
        out_specs=P("tensor", "dp", None, None),
        check_vma=False,
    )
```

```python
import functools

import jax
import jax.numpy as jnp
import numpy as np
from jax import lax
from jax.experimental import pallas as pl
from jax.experimental.pallas import tpu as pltpu
from jax.sharding import PartitionSpec as P

VMEM = pl.BlockSpec(memory_space=pltpu.VMEM)
SMEM = pl.BlockSpec(memory_space=pltpu.SMEM)
BF16 = jnp.bfloat16
F32 = jnp.float32


def call(body, name, outs, in_specs, args, flops=0, scratch=()):
    moved = sum(int(np.prod(o.shape)) * o.dtype.itemsize for o in outs)
    moved += sum(int(np.prod(a.shape)) * a.dtype.itemsize for a in args)
    return pl.pallas_call(
        body,
        name=name,
        out_shape=tuple(outs),
        in_specs=in_specs,
        out_specs=tuple(VMEM for _ in outs),
        scratch_shapes=list(scratch),
        compiler_params=pltpu.CompilerParams(vmem_limit_bytes=40 << 20),
        cost_estimate=pl.CostEstimate(flops=flops, bytes_accessed=moved, transcendentals=0),
    )(*args)


def swap(value, axis, bit):
    size = lax.axis_size(axis)
    return lax.ppermute(value, axis, [(i, i ^ (1 << bit)) for i in range(size)])


def spread(value):
    parts = [value[None]]
    for bit in range(lax.axis_size("tensor").bit_length() - 1):
        whole = parts[0] if len(parts) == 1 else jnp.concatenate(parts, 0)
        parts.append(swap(whole, "tensor", bit))
    return parts


def split_masters(masters, tokens, low, high):
    del tokens
    half = low.shape[1]
    for block in range(masters.shape[1]):
        turned = masters[0, block].T.astype(BF16)
        low[block], high[block] = turned[:half], turned[half:]


def split_upstream(place, grad, kept, *refs):
    parts, blocks, arrived = refs[:-2], refs[-2], refs[-1]
    count, half, side = kept.shape[0], kept.shape[1], kept.shape[2]

    def fetch(k):
        start = pl.multiple_of(place[3 + count + k] * side, side)
        return pltpu.make_async_copy(grad.at[:, pl.ds(start, side)], blocks.at[k], arrived.at[k])

    for k in range(count):
        fetch(k).start()
    for k in range(count):
        fetch(k).wait()
        turned = blocks[k].T
        low, high = turned[:half], turned[half:]
        swapped = place[0] != 0
        kept[k] = jnp.where(swapped, high, low)
        sent = jnp.where(swapped, low, high)
        start = 0
        for part in parts:
            part[k] = sent[start : start + part.shape[1]]
            start += part.shape[1]


def select_rows(first, place, *refs):
    sources, before, chosen = refs[:-1], None, refs[-1]
    side = chosen.shape[2]
    per_shard = sources[0].shape[2] // side
    for k in range(chosen.shape[0]):
        shard = place[3 + k] // per_shard
        start = pl.multiple_of((place[3 + k] - shard * per_shard) * side, side)
        offset = shard ^ place[1]
        value, at = None if first == 0 else before[k], first
        for source in sources:
            size = source.shape[0]
            here = source[jnp.clip(offset - at, 0, size - 1), :, pl.ds(start, side)]
            value = here if value is None else jnp.where(offset >= at, here, value)
            at += size
        chosen[k] = value


def add_duplicates(first, table, total):
    for k in range(1, total.shape[0]):

        @pl.when(table[first, k] != k)
        def _():
            total[table[first, k]] += total[k]


def slopes(gate, up):
    sigmoid = 0.5 + 0.5 * jnp.tanh(0.5 * gate)
    return sigmoid * up * (1.0 + gate * (1.0 - sigmoid)), sigmoid * gate


def project(weight, source):
    return lax.dot_general(weight, source, (((1,), (1,)), ((), ())), preferred_element_type=F32)


def term(upstream, gate_slope, up_slope, source):
    upstream = upstream.astype(F32)
    both = [(upstream * gate_slope).astype(BF16), (upstream * up_slope).astype(BF16)]
    return jnp.dot(jnp.concatenate(both, axis=0), source, preferred_element_type=F32)


def own_part(rows, table, *refs):
    sources, own_tokens, own_up, weights, grad, total = refs[:4], refs[4], refs[5], refs[6], refs[7], refs[8]
    places, half = own_up.shape[0], own_up.shape[1]
    position = 0
    for source in sources:
        for p in range(source.shape[0]):
            block = table[rows["order"], position + p]
            up = (block >= places).astype(jnp.int32)
            weights[block - up * places, pl.ds(pl.multiple_of(up * half, half), half), :] = source[p]
        position += source.shape[0]
    for k in range(places):
        total[k] = project(weights[k], own_tokens[k])
    add_duplicates(rows["first"], table, total)
    for k in range(places):
        first = table[rows["first"], k]
        grad[k] = term(own_up[k], *slopes(total[first, :half], total[first, half:]), own_tokens[k])


def other_slopes(rows, plan, weights, other_tokens, slope, table, arrived, total):
    places, half = weights.shape[0], weights.shape[1] // 2
    copy = pltpu.make_async_copy(plan, table, arrived)
    copy.start()
    for k in range(places):
        total[k] = project(weights[k], other_tokens[k])
    copy.wait()
    add_duplicates(rows["first"], table, total)
    for k in range(places):
        first = table[rows["first"], k]
        slope[k, :half], slope[k, half:] = slopes(total[first, :half], total[first, half:])


def scalar(table, row):
    return jnp.max(table[pl.ds(row, 1), :].astype(F32)).astype(jnp.int32)


def other_part(rows, steps, start, plan, slope, other_tokens, other_up, grad, *refs):
    outs, (table, arrived, total, *ordered) = refs[: 2 * len(steps)], refs[2 * len(steps) :]
    copy = pltpu.make_async_copy(plan, table, arrived)
    copy.start()
    places, height, half = other_up.shape[0], other_up.shape[1], grad.shape[1] // 2
    gate, up = pl.ds(start, height), pl.ds(half + start, height)
    for k in range(places):
        result = term(other_up[k], slope[k, gate], slope[k, up], other_tokens[k])
        total[k, :height] = grad[k, gate] + result[:height]
        total[k, height:] = grad[k, up] + result[height:]
    copy.wait()
    first = 0
    for n, (order, step) in enumerate(steps):
        sent, kept = outs[2 * n], outs[2 * n + 1]
        room, size = sent.shape[0], sent.shape[1]
        for block in range(2 * places):
            which, k = divmod(block, places)
            ordered[n][table[rows[order, "at"], block]] = total[k, pl.ds(which * height + first, size), :]
        sent[...] = ordered[n][pl.ds(table[rows[step, "sent"], 0], room)].astype(BF16)
        kept[...] = ordered[n][pl.ds(table[rows[step, "kept"], 0], room)]
        first += size


def combine(sent_row, kept_row, pieces, table, *refs):
    kept_in, received, (sent, kept, total) = refs[:pieces], refs[pieces : 2 * pieces], refs[2 * pieces :]
    count, room, start = kept_in[0].shape[0], sent.shape[0], 0
    for mine, other in zip(kept_in, received):
        total[:count, start : start + mine.shape[1]] = mine[...] + other[...].astype(F32)
        start += mine.shape[1]
    sent[...] = total[pl.ds(jnp.minimum(scalar(table, sent_row), count), room)].astype(BF16)
    kept[...] = total[pl.ds(jnp.minimum(scalar(table, kept_row), count), room)]


def finish(count_row, pair_row, table, *refs):
    ends, out = refs[:-1], refs[-1]
    count, swapped = scalar(table, count_row), scalar(table, pair_row) != 0
    for slot in range(out.shape[1]):
        mine = jnp.concatenate([end[slot] for end in ends[0::2]], axis=0)
        other = jnp.concatenate([end[slot] for end in ends[1::2]], axis=0).astype(F32)
        low, high = jnp.where(swapped, other, mine), jnp.where(swapped, mine, other)
        whole = jnp.concatenate([low, high], axis=0).T
        out[0, slot] = jnp.where(slot < count, whole, 0.0)


def axes_of(owner_count):
    bits = owner_count.bit_length() - 1
    if bits == 4:
        y, near, far = 1, 2, 3
        parts = ((1, (near, y, far)), (1, (y, far, near))), ((1, (near, y, far)), (1, (y, near, far)))
        turns = tuple(((part,), 0) for part in range(2)) + tuple(((piece,), n) for n in range(1, 4) for piece in range(4))
        return 0, (y, near), (far,), parts, turns
    pair, ends, rest = bits - 2, (0, bits - 1), tuple(range(1, bits - 2))
    parts = ((2, (*ends, *rest)),), ((2, (*ends[::-1], *rest)),)
    return pair, ends, rest, parts, tuple(((piece,), n) for n in range(bits) for piece in range(2))


def orders_of(axes):
    return list(dict.fromkeys((*order, axes[0]) for part in axes[3] for _, order in part))


def steps_of(axes):
    return list(dict.fromkeys((tuple(sorted(o[:n])), bit) for o in orders_of(axes) for n, bit in enumerate(o)))


def rows_of(axes):
    names = ["order", "first", "end", "pair", "fits"]
    names += [(order, "at") for order in orders_of(axes)]
    names += [(step, kind) for step in steps_of(axes) for kind in ("sent", "kept")]
    return {name: n for n, name in enumerate(names)}


def make_plan(axes, usual, own_blocks, place, columns, found, *refs):
    pair, rows, owners, table = axes[0], rows_of(axes), refs[:-1], refs[-1]
    count, places = owners[0].shape[1], columns.shape[1]
    me = place[2]
    across = lax.broadcasted_iota(jnp.int32, (count, count), 1)
    down = lax.broadcasted_iota(jnp.int32, (count, count), 0)
    owner_row, column_row = owners[0][...], columns[...]

    def as_column(row):
        size = row.shape[1]
        kept = jnp.where((across == down)[:size, :size], row.astype(F32), 0.0)
        return jnp.sum(kept, axis=1, keepdims=True).astype(jnp.int32)

    def number(mask):
        return jnp.where(mask, 1.0, 0.0)

    def write(name, row):
        table[pl.ds(rows[name], 1), :] = jnp.broadcast_to(row, (1, count)).astype(jnp.int32)

    owner_col, column_col = as_column(owner_row), as_column(column_row)
    table[...] = jnp.zeros(table.shape, jnp.int32)
    write("order", (found[0:1, :] ^ me) * own_blocks + found[1:2, :])
    same = column_row == column_col
    place_at = lax.broadcasted_iota(jnp.int32, (places, places), 0).astype(F32)
    first = jnp.min(jnp.where(same, place_at, float(places)), axis=0, keepdims=True)
    table[pl.ds(rows["first"], 1), :places] = first.astype(jnp.int32)
    write("pair", jnp.full((1, 1), (me >> pair) & 1, jnp.int32))
    for order in orders_of(axes):

        def key(owner):
            return sum(((owner >> bit) & 1) << n for n, bit in enumerate(order[::-1]))

        ahead = key(owner_col) < key(owner_row)
        ahead = jnp.logical_or(ahead, jnp.logical_and(key(owner_col) == key(owner_row), down < across))
        write((order, "at"), jnp.sum(number(ahead), axis=0, keepdims=True))

    def alive(done):
        return ((owner_row ^ me) & sum(1 << b for b in done)) == 0

    for step in steps_of(axes):
        done, bit = step
        low = jnp.logical_and(alive(done), ((owner_row >> bit) & 1) == 0)
        total, mine = jnp.sum(number(low), axis=1, keepdims=True), ((me >> bit) & 1).astype(F32)
        write((step, "sent"), total * (1.0 - mine))
        write((step, "kept"), total * mine)
    everything = alive((*axes[1], *axes[2], pair))
    write("end", jnp.sum(number(everything), axis=1, keepdims=True))
    over = jnp.zeros((1, 1), F32)
    for row in [part[n : n + 1, :] for part in owners for n in range(part.shape[0])]:
        column = as_column(row)
        for done, most in usual.items():
            mask = sum(1 << b for b in done)
            group = (row & mask) == (column & mask)
            taken = jnp.max(jnp.sum(number(group), axis=1, keepdims=True), axis=0, keepdims=True)
            over = jnp.maximum(over, taken - most)
    write("fits", number(over <= 0.0))


def local(tokens, hidden_grad, masters, block_row, block_col, owners):
    owner_count = lax.axis_size("dp")
    me = lax.axis_index("dp")
    axes = axes_of(owner_count)
    pair, (bit_a, bit_b), rest, parts, turns = axes
    own_blocks, side = masters.shape[1], masters.shape[2]
    places, half, quarter = block_row.shape[1], side // 2, side // 8
    block_count = owners.shape[1]
    token_count = tokens.shape[0]
    capacity = 3 * block_count // owner_count
    place = jnp.stack([(me >> pair) & 1, lax.axis_index("tensor"), me]).astype(jnp.int32)
    place = jnp.concatenate([place, block_row[0], block_col[0]])

    def struct(shape, dtype):
        return jax.ShapeDtypeStruct(shape, dtype)

    with jax.named_scope("tokens"):
        all_owners = [part.reshape(-1, block_count) for part in spread(owners)]
        own_chosen = call(
            functools.partial(select_rows, 0), "select_rows", [struct((places, token_count, side), BF16)],
            [SMEM] + [VMEM] * lax.axis_size("tensor").bit_length(), [place, *spread(tokens)],
        )[0]

    with jax.named_scope("weights"):
        low, high = call(
            split_masters, "split_masters", [struct((own_blocks, half, side), BF16)] * 2, [VMEM] * 2, [masters, tokens]
        )
        upper = ((me >> pair) & 1) == 1
        kept, sent = jnp.where(upper, high, low), jnp.where(upper, low, high)
        entries = [(0, b) for b in range(own_blocks)]

        def moved(found, bit):
            return [(delta ^ (1 << bit), b) for delta, b in found]

        got = swap(sent, "dp", pair)
        entries = entries + moved(entries, pair)
        later, got = lax.optimization_barrier((place, got))
        other_chosen = swap(own_chosen, "dp", pair)
        current = jnp.concatenate([kept, got], 0)
        for bit in rest[:0:-1]:
            current = jnp.concatenate([current, swap(current, "dp", bit)], 0)
            entries = entries + moved(entries, bit)
        far = swap(current, "dp", rest[0])
        heights = [sum(share for share, _ in part) * quarter for part in parts]
        own_up, *sent_up = call(
            split_upstream, "split_upstream",
            [struct((places, height, token_count), BF16) for height in (half, *heights)],
            [SMEM, pl.BlockSpec(memory_space=pltpu.HBM)], [later, hidden_grad], 0,
            [pltpu.VMEM((places, token_count, side), BF16), pltpu.SemaphoreType.DMA((places,))],
        )
        current, far, sent_up = lax.optimization_barrier((current, far, sent_up))
        near_a, near_b = swap(current, "dp", bit_a), swap(far, "dp", bit_b)
        entries_a, entries_b = entries + moved(entries, bit_a), moved(entries, rest[0])
        entries_b = entries_b + moved(entries_b, bit_b)
        found = entries_a + moved(entries_a, bit_b) + entries_b + moved(entries_b, bit_a)
        found = np.array(found, np.int32).T

    with jax.named_scope("plan"):

        def most_of(done):
            return min(block_count, (owner_count >> len(done)) * capacity)

        def load_of(done):
            return min(most_of(done), (block_count >> len(done)) + capacity + (len(done) < 3))

        rows = rows_of(axes)
        settled = [tuple(sorted((*done, bit))) for done, bit in steps_of(axes)]
        usual = {done: load_of(done) for done in settled if load_of(done) < most_of(done)}
        table = call(
            functools.partial(make_plan, axes, usual, own_blocks), "make_plan",
            [struct((-(-len(rows) // 8) * 8, block_count), jnp.int32)], [SMEM] + [VMEM] * (2 + len(all_owners)),
            [later, block_col, jnp.asarray(found), *all_owners],
        )[0]

    with jax.named_scope("weights"):
        near_a, near_b, table = lax.optimization_barrier((near_a, near_b, table))
        a0, b0 = jnp.concatenate([current, near_a], 0), jnp.concatenate([far, near_b], 0)
        a1, b1 = swap(a0, "dp", bit_b), swap(b0, "dp", bit_a)

    with jax.named_scope("upstream"):
        other_up = [swap(sent, "dp", pair) for sent in sent_up]

    work = 2 * 2 * places * side * side * token_count
    with jax.named_scope("own_tokens"):
        weights, grad = call(
            functools.partial(own_part, rows), "own_part",
            [struct((places, side, side), BF16), struct((places, side, side), F32)], [SMEM] + [VMEM] * 6,
            [table, a0, a1, b0, b1, own_chosen, own_up], work, [pltpu.VMEM((places, side, token_count), F32)],
        )
    with jax.named_scope("other_tokens"):
        slope = call(
            functools.partial(other_slopes, rows), "other_slopes", [struct((places, side, token_count), F32)],
            [VMEM] * 3, [table, weights, other_chosen], work // 2,
            [pltpu.SMEM(table.shape, jnp.int32), pltpu.SemaphoreType.DMA, pltpu.VMEM((places, side, token_count), F32)],
        )[0]

    def reduce(load, table, slope, other_chosen, other_up, grad):
        orders, firsts, start = [], [], 0
        for part in parts:
            firsts.append((len(orders), start))
            orders += [(*order, pair) for _, order in part]
            start += sum(share for share, _ in part) * quarter
        state, turn = {}, None
        for group, n in turns:
            order = orders[group[0]]
            if n == 0:
                (at,) = group
                part, up, (piece, start) = parts[at], other_up[at], firsts[at]
                steps = [((*order, pair), ((), order[0])) for _, order in part]
                shapes = [(load(order[:1]), share * quarter, side) for share, order in part]
                body, spec = functools.partial(other_part, rows, steps, start), [VMEM] * 5
                args = [table, slope, other_chosen, up, grad]
                scratch = [pltpu.SMEM(table.shape, jnp.int32), pltpu.SemaphoreType.DMA]
                scratch += [pltpu.VMEM((places, 2 * up.shape[1], side), F32)]
                scratch += [pltpu.VMEM((block_count + room, *rest_of), F32) for room, *rest_of in shapes]
                made = [(piece + i,) for i in range(len(part))]
            else:
                joined = [state.pop(key) for key in sorted(state) if set(key) <= set(group)]
                step = tuple(sorted(order[:n])), order[n]
                body = functools.partial(combine, rows[step, "sent"], rows[step, "kept"], len(joined))
                room, was, height = load(order[: n + 1]), joined[0][0].shape[0], sum(k.shape[1] for k, _ in joined)
                shapes, spec = [(room, height, side)], [VMEM] * (1 + 2 * len(joined))
                args = [table, *(k for k, _ in joined), *(g for _, g in joined)]
                scratch, made = [pltpu.VMEM((was + room, height, side), F32)], [group]
            if turn is not None:
                args[-1], _ = lax.optimization_barrier((args[-1], turn))
            outs = call(
                body, "combine" if n else "other_part", [struct(shape, dtype) for shape in shapes for dtype in (BF16, F32)],
                spec, args, 0 if n else work // 4, scratch,
            )
            turn = outs[1]
            for key, sent, kept in zip(made, outs[0::2], outs[1::2]):
                state[key] = kept, swap(sent, "dp", orders[key[0]][n])
        return [end for key in sorted(state) for end in state[key]]

    operands = (table, slope, other_chosen, other_up, grad)
    ends = reduce(load_of, *operands)
    ends = lax.cond(table[rows["fits"], 0] == 1, lambda ends, operands: ends, lambda ends, operands: reduce(most_of, *operands), ends, operands)
    return call(
        functools.partial(finish, rows["end"], rows["pair"]), "finish", [struct((1, capacity, side, side), F32)],
        [VMEM] * (1 + len(ends)), [table, *ends],
    )[0]


def solution(mesh):
    return jax.shard_map(
        local,
        mesh=mesh,
        in_specs=(
            P("dp", "tensor"),
            P("dp", "tensor"),
            P("tensor", "dp", None, None),
            P("tensor", None),
            P("tensor", None),
            P("tensor", None),
        ),
        out_specs=P("tensor", "dp", None, None),
        check_vma=False,
    )
```

```python
import functools

import jax
import jax.numpy as jnp
import numpy as np
from jax import lax
from jax.experimental import pallas as pl
from jax.experimental.pallas import tpu as pltpu
from jax.sharding import PartitionSpec as P

VMEM = pl.BlockSpec(memory_space=pltpu.VMEM)
SMEM = pl.BlockSpec(memory_space=pltpu.SMEM)
BF16 = jnp.bfloat16
F32 = jnp.float32


def call(body, name, outs, in_specs, args, flops=0, scratch=()):
    moved = sum(int(np.prod(o.shape)) * o.dtype.itemsize for o in outs)
    moved += sum(int(np.prod(a.shape)) * a.dtype.itemsize for a in args)
    return pl.pallas_call(
        body,
        name=name,
        out_shape=tuple(outs),
        in_specs=in_specs,
        out_specs=tuple(VMEM for _ in outs),
        scratch_shapes=list(scratch),
        compiler_params=pltpu.CompilerParams(vmem_limit_bytes=40 << 20),
        cost_estimate=pl.CostEstimate(flops=flops, bytes_accessed=moved, transcendentals=0),
    )(*args)


def swap(value, axis, bit):
    size = lax.axis_size(axis)
    return lax.ppermute(value, axis, [(i, i ^ (1 << bit)) for i in range(size)])


def spread(value):
    parts = [value[None]]
    for bit in range(lax.axis_size("tensor").bit_length() - 1):
        whole = parts[0] if len(parts) == 1 else jnp.concatenate(parts, 0)
        parts.append(swap(whole, "tensor", bit))
    return parts


def split_masters(masters, tokens, low, high):
    del tokens
    half = low.shape[1]
    for block in range(masters.shape[1]):
        turned = masters[0, block].T.astype(BF16)
        low[block], high[block] = turned[:half], turned[half:]


def split_upstream(place, grad, kept, *refs):
    parts, blocks, arrived = refs[:-2], refs[-2], refs[-1]
    count, half, side = kept.shape[0], kept.shape[1], kept.shape[2]

    def fetch(k):
        start = pl.multiple_of(place[3 + count + k] * side, side)
        return pltpu.make_async_copy(grad.at[:, pl.ds(start, side)], blocks.at[k], arrived.at[k])

    for k in range(count):
        fetch(k).start()
    for k in range(count):
        fetch(k).wait()
        turned = blocks[k].T
        low, high = turned[:half], turned[half:]
        swapped = place[0] != 0
        kept[k] = jnp.where(swapped, high, low)
        sent = jnp.where(swapped, low, high)
        start = 0
        for part in parts:
            part[k] = sent[start : start + part.shape[1]]
            start += part.shape[1]


def select_rows(first, place, *refs):
    sources, before, chosen = refs[:-1], None, refs[-1]
    side = chosen.shape[2]
    per_shard = sources[0].shape[2] // side
    for k in range(chosen.shape[0]):
        shard = place[3 + k] // per_shard
        start = pl.multiple_of((place[3 + k] - shard * per_shard) * side, side)
        offset = shard ^ place[1]
        value, at = None if first == 0 else before[k], first
        for source in sources:
            size = source.shape[0]
            here = source[jnp.clip(offset - at, 0, size - 1), :, pl.ds(start, side)]
            value = here if value is None else jnp.where(offset >= at, here, value)
            at += size
        chosen[k] = value


def add_duplicates(first, table, total):
    for k in range(1, total.shape[0]):

        @pl.when(table[first, k] != k)
        def _():
            total[table[first, k]] += total[k]


def slopes(gate, up):
    sigmoid = 0.5 + 0.5 * jnp.tanh(0.5 * gate)
    return sigmoid * up * (1.0 + gate * (1.0 - sigmoid)), sigmoid * gate


def project(weight, source):
    return lax.dot_general(weight, source, (((1,), (1,)), ((), ())), preferred_element_type=F32)


def term(upstream, gate_slope, up_slope, source):
    upstream = upstream.astype(F32)
    both = [(upstream * gate_slope).astype(BF16), (upstream * up_slope).astype(BF16)]
    return jnp.dot(jnp.concatenate(both, axis=0), source, preferred_element_type=F32)


def own_part(rows, table, *refs):
    sources, own_tokens, own_up, weights, grad, total = refs[:4], refs[4], refs[5], refs[6], refs[7], refs[8]
    places, half = own_up.shape[0], own_up.shape[1]
    position = 0
    for source in sources:
        for p in range(source.shape[0]):
            block = table[rows["order"], position + p]
            up = (block >= places).astype(jnp.int32)
            weights[block - up * places, pl.ds(pl.multiple_of(up * half, half), half), :] = source[p]
        position += source.shape[0]
    for k in range(places):
        total[k] = project(weights[k], own_tokens[k])
    add_duplicates(rows["first"], table, total)
    for k in range(places):
        first = table[rows["first"], k]
        grad[k] = term(own_up[k], *slopes(total[first, :half], total[first, half:]), own_tokens[k])


def other_slopes(rows, table, weights, other_tokens, slope, total):
    places, half = weights.shape[0], weights.shape[1] // 2
    for k in range(places):
        total[k] = project(weights[k], other_tokens[k])
    add_duplicates(rows["first"], table, total)
    for k in range(places):
        first = table[rows["first"], k]
        slope[k, :half], slope[k, half:] = slopes(total[first, :half], total[first, half:])


def scalar(table, row):
    return jnp.max(table[pl.ds(row, 1), :].astype(F32)).astype(jnp.int32)


def other_part(rows, steps, start, plan, slope, other_tokens, other_up, grad, *refs):
    outs, (table, arrived, total, *ordered) = refs[: 2 * len(steps)], refs[2 * len(steps) :]
    copy = pltpu.make_async_copy(plan, table, arrived)
    copy.start()
    places, height, half = other_up.shape[0], other_up.shape[1], grad.shape[1] // 2
    gate, up = pl.ds(start, height), pl.ds(half + start, height)
    for k in range(places):
        result = term(other_up[k], slope[k, gate], slope[k, up], other_tokens[k])
        total[k, :height] = grad[k, gate] + result[:height]
        total[k, height:] = grad[k, up] + result[height:]
    copy.wait()
    first = 0
    for n, (order, step) in enumerate(steps):
        sent, kept = outs[2 * n], outs[2 * n + 1]
        room, size = sent.shape[0], sent.shape[1]
        for block in range(2 * places):
            which, k = divmod(block, places)
            ordered[n][table[rows[order, "at"], block]] = total[k, pl.ds(which * height + first, size), :]
        sent[...] = ordered[n][pl.ds(table[rows[step, "sent"], 0], room)].astype(BF16)
        kept[...] = ordered[n][pl.ds(table[rows[step, "kept"], 0], room)]
        first += size


def combine(sent_row, kept_row, pieces, table, *refs):
    kept_in, received, (sent, kept, total) = refs[:pieces], refs[pieces : 2 * pieces], refs[2 * pieces :]
    count, room, start = kept_in[0].shape[0], sent.shape[0], 0
    for mine, other in zip(kept_in, received):
        total[:count, start : start + mine.shape[1]] = mine[...] + other[...].astype(F32)
        start += mine.shape[1]
    sent[...] = total[pl.ds(jnp.minimum(scalar(table, sent_row), count), room)].astype(BF16)
    kept[...] = total[pl.ds(jnp.minimum(scalar(table, kept_row), count), room)]


def turn_own(count_row, pair_row, table, *refs):
    ends, out = refs[:-1], refs[-1]
    count, swapped = scalar(table, count_row), scalar(table, pair_row) != 0
    for slot in range(out.shape[0]):
        mine = jnp.concatenate([end[slot] for end in ends], axis=0)
        mine = jnp.where(slot < count, mine, 0.0)
        zero = jnp.zeros(mine.shape, F32)
        low, high = jnp.where(swapped, zero, mine), jnp.where(swapped, mine, zero)
        out[slot] = jnp.concatenate([low, high], axis=0).T


def finish(count_row, pair_row, table, own, *refs):
    ends, out = refs[:-1], refs[-1]
    count, swapped = scalar(table, count_row), scalar(table, pair_row) != 0
    half = sum(end.shape[1] for end in ends)
    high = (lax.broadcasted_iota(jnp.int32, out.shape[2:], 1) >= half) != swapped
    for slot in range(out.shape[1]):
        other = jnp.concatenate([end[slot] for end in ends], axis=0).astype(F32).T
        other = jnp.concatenate([other, other], axis=1)
        out[0, slot] = jnp.where(jnp.logical_and(slot < count, high), other, own[slot])


def axes_of(owner_count):
    bits = owner_count.bit_length() - 1
    if bits == 4:
        y, near, far = 1, 2, 3
        parts = ((1, (near, y, far)), (1, (y, far, near))), ((1, (near, y, far)), (1, (y, near, far)))
        turns = tuple(((part,), 0) for part in range(2)) + tuple(((piece,), n) for n in range(1, 4) for piece in range(4))
        return 0, (y, near), (far,), parts, turns
    pair, ends, rest = bits - 2, (0, bits - 1), tuple(range(1, bits - 2))
    parts = ((2, (*ends, *rest)),), ((2, (*ends[::-1], *rest)),)
    return pair, ends, rest, parts, tuple(((piece,), n) for n in range(bits) for piece in range(2))


def orders_of(axes):
    return list(dict.fromkeys((*order, axes[0]) for part in axes[3] for _, order in part))


def steps_of(axes):
    return list(dict.fromkeys((tuple(sorted(o[:n])), bit) for o in orders_of(axes) for n, bit in enumerate(o)))


def rows_of(axes):
    names = ["order", "first", "end", "pair", "fits"]
    names += [(order, "at") for order in orders_of(axes)]
    names += [(step, kind) for step in steps_of(axes) for kind in ("sent", "kept")]
    return {name: n for n, name in enumerate(names)}


def make_plan(axes, usual, own_blocks, place, columns, found, *refs):
    pair, rows, owners, table = axes[0], rows_of(axes), refs[:-1], refs[-1]
    count, places = owners[0].shape[1], columns.shape[1]
    me = place[2]
    across = lax.broadcasted_iota(jnp.int32, (count, count), 1)
    down = lax.broadcasted_iota(jnp.int32, (count, count), 0)
    owner_row, column_row = owners[0][...], columns[...]

    def as_column(row):
        size = row.shape[1]
        kept = jnp.where((across == down)[:size, :size], row.astype(F32), 0.0)
        return jnp.sum(kept, axis=1, keepdims=True).astype(jnp.int32)

    def number(mask):
        return jnp.where(mask, 1.0, 0.0)

    def write(name, row):
        table[pl.ds(rows[name], 1), :] = jnp.broadcast_to(row, (1, count)).astype(jnp.int32)

    owner_col, column_col = as_column(owner_row), as_column(column_row)
    table[...] = jnp.zeros(table.shape, jnp.int32)
    write("order", (found[0:1, :] ^ me) * own_blocks + found[1:2, :])
    same = column_row == column_col
    place_at = lax.broadcasted_iota(jnp.int32, (places, places), 0).astype(F32)
    first = jnp.min(jnp.where(same, place_at, float(places)), axis=0, keepdims=True)
    table[pl.ds(rows["first"], 1), :places] = first.astype(jnp.int32)
    write("pair", jnp.full((1, 1), (me >> pair) & 1, jnp.int32))
    for order in orders_of(axes):

        def key(owner):
            return sum(((owner >> bit) & 1) << n for n, bit in enumerate(order[::-1]))

        ahead = key(owner_col) < key(owner_row)
        ahead = jnp.logical_or(ahead, jnp.logical_and(key(owner_col) == key(owner_row), down < across))
        write((order, "at"), jnp.sum(number(ahead), axis=0, keepdims=True))

    def alive(done):
        return ((owner_row ^ me) & sum(1 << b for b in done)) == 0

    for step in steps_of(axes):
        done, bit = step
        low = jnp.logical_and(alive(done), ((owner_row >> bit) & 1) == 0)
        total, mine = jnp.sum(number(low), axis=1, keepdims=True), ((me >> bit) & 1).astype(F32)
        write((step, "sent"), total * (1.0 - mine))
        write((step, "kept"), total * mine)
    everything = alive((*axes[1], *axes[2], pair))
    write("end", jnp.sum(number(everything), axis=1, keepdims=True))
    over = jnp.zeros((1, 1), F32)
    for row in [part[n : n + 1, :] for part in owners for n in range(part.shape[0])]:
        column = as_column(row)
        for done, most in usual.items():
            mask = sum(1 << b for b in done)
            group = (row & mask) == (column & mask)
            taken = jnp.max(jnp.sum(number(group), axis=1, keepdims=True), axis=0, keepdims=True)
            over = jnp.maximum(over, taken - most)
    write("fits", number(over <= 0.0))


def local(tokens, hidden_grad, masters, block_row, block_col, owners):
    owner_count = lax.axis_size("dp")
    me = lax.axis_index("dp")
    axes = axes_of(owner_count)
    pair, (bit_a, bit_b), rest, parts, turns = axes
    own_blocks, side = masters.shape[1], masters.shape[2]
    places, half, quarter = block_row.shape[1], side // 2, side // 8
    block_count = owners.shape[1]
    token_count = tokens.shape[0]
    capacity = 3 * block_count // owner_count
    place = jnp.stack([(me >> pair) & 1, lax.axis_index("tensor"), me]).astype(jnp.int32)
    place = jnp.concatenate([place, block_row[0], block_col[0]])

    def struct(shape, dtype):
        return jax.ShapeDtypeStruct(shape, dtype)

    with jax.named_scope("tokens"):
        all_owners = [part.reshape(-1, block_count) for part in spread(owners)]
        own_chosen = call(
            functools.partial(select_rows, 0), "select_rows", [struct((places, token_count, side), BF16)],
            [SMEM] + [VMEM] * lax.axis_size("tensor").bit_length(), [place, *spread(tokens)],
        )[0]

    with jax.named_scope("weights"):
        low, high = call(
            split_masters, "split_masters", [struct((own_blocks, half, side), BF16)] * 2, [VMEM] * 2, [masters, tokens]
        )
        upper = ((me >> pair) & 1) == 1
        kept, sent = jnp.where(upper, high, low), jnp.where(upper, low, high)
        entries = [(0, b) for b in range(own_blocks)]

        def moved(found, bit):
            return [(delta ^ (1 << bit), b) for delta, b in found]

        got = swap(sent, "dp", pair)
        entries = entries + moved(entries, pair)
        later, got = lax.optimization_barrier((place, got))
        other_chosen = swap(own_chosen, "dp", pair)
        current = jnp.concatenate([kept, got], 0)
        for bit in rest[:0:-1]:
            current = jnp.concatenate([current, swap(current, "dp", bit)], 0)
            entries = entries + moved(entries, bit)
        far = swap(current, "dp", rest[0])
        heights = [sum(share for share, _ in part) * quarter for part in parts]
        own_up, *sent_up = call(
            split_upstream, "split_upstream",
            [struct((places, height, token_count), BF16) for height in (half, *heights)],
            [SMEM, pl.BlockSpec(memory_space=pltpu.HBM)], [later, hidden_grad], 0,
            [pltpu.VMEM((places, token_count, side), BF16), pltpu.SemaphoreType.DMA((places,))],
        )
        current, far, sent_up = lax.optimization_barrier((current, far, sent_up))
        near_a, near_b = swap(current, "dp", bit_a), swap(far, "dp", bit_b)
        entries_a, entries_b = entries + moved(entries, bit_a), moved(entries, rest[0])
        entries_b = entries_b + moved(entries_b, bit_b)
        found = entries_a + moved(entries_a, bit_b) + entries_b + moved(entries_b, bit_a)
        found = np.array(found, np.int32).T

    with jax.named_scope("plan"):

        def most_of(done):
            return min(block_count, (owner_count >> len(done)) * capacity)

        def load_of(done):
            return min(most_of(done), (block_count >> len(done)) + capacity)

        rows = rows_of(axes)
        settled = [tuple(sorted((*done, bit))) for done, bit in steps_of(axes)]
        usual = {done: load_of(done) for done in settled if load_of(done) < most_of(done)}
        table = call(
            functools.partial(make_plan, axes, usual, own_blocks), "make_plan",
            [struct((-(-len(rows) // 8) * 8, block_count), jnp.int32)], [SMEM] + [VMEM] * (2 + len(all_owners)),
            [later, block_col, jnp.asarray(found), *all_owners],
        )[0]

    with jax.named_scope("weights"):
        near_a, near_b, table = lax.optimization_barrier((near_a, near_b, table))
        a0, b0 = jnp.concatenate([current, near_a], 0), jnp.concatenate([far, near_b], 0)
        a1, b1 = swap(a0, "dp", bit_b), swap(b0, "dp", bit_a)

    with jax.named_scope("upstream"):
        other_up = [swap(sent, "dp", pair) for sent in sent_up]

    work = 2 * 2 * places * side * side * token_count
    with jax.named_scope("own_tokens"):
        weights, grad = call(
            functools.partial(own_part, rows), "own_part",
            [struct((places, side, side), BF16), struct((places, side, side), F32)], [SMEM] + [VMEM] * 6,
            [table, a0, a1, b0, b1, own_chosen, own_up], work, [pltpu.VMEM((places, side, token_count), F32)],
        )
    with jax.named_scope("other_tokens"):
        slope = call(
            functools.partial(other_slopes, rows), "other_slopes", [struct((places, side, token_count), F32)],
            [SMEM, VMEM, VMEM], [table, weights, other_chosen], work // 2,
            [pltpu.VMEM((places, side, token_count), F32)],
        )[0]

    def reduce(load, table, slope, other_chosen, other_up, grad):
        orders, firsts, start = [], [], 0
        for part in parts:
            firsts.append((len(orders), start))
            orders += [(*order, pair) for _, order in part]
            start += sum(share for share, _ in part) * quarter
        state, turn = {}, None
        for group, n in turns:
            order = orders[group[0]]
            if n == 0:
                (at,) = group
                part, up, (piece, start) = parts[at], other_up[at], firsts[at]
                steps = [((*order, pair), ((), order[0])) for _, order in part]
                shapes = [(load(order[:1]), share * quarter, side) for share, order in part]
                body, spec = functools.partial(other_part, rows, steps, start), [VMEM] * 5
                args = [table, slope, other_chosen, up, grad]
                scratch = [pltpu.SMEM(table.shape, jnp.int32), pltpu.SemaphoreType.DMA]
                scratch += [pltpu.VMEM((places, 2 * up.shape[1], side), F32)]
                scratch += [pltpu.VMEM((block_count + room, *rest_of), F32) for room, *rest_of in shapes]
                made = [(piece + i,) for i in range(len(part))]
            else:
                joined = [state.pop(key) for key in sorted(state) if set(key) <= set(group)]
                step = tuple(sorted(order[:n])), order[n]
                body = functools.partial(combine, rows[step, "sent"], rows[step, "kept"], len(joined))
                room, was, height = load(order[: n + 1]), joined[0][0].shape[0], sum(k.shape[1] for k, _ in joined)
                shapes, spec = [(room, height, side)], [VMEM] * (1 + 2 * len(joined))
                args = [table, *(k for k, _ in joined), *(g for _, g in joined)]
                scratch, made = [pltpu.VMEM((was + room, height, side), F32)], [group]
            if turn is not None:
                args[-1], _ = lax.optimization_barrier((args[-1], turn))
            outs = call(
                body, "combine" if n else "other_part", [struct(shape, dtype) for shape in shapes for dtype in (BF16, F32)],
                spec, args, 0 if n else work // 4, scratch,
            )
            turn = outs[1]
            for key, sent, kept in zip(made, outs[0::2], outs[1::2]):
                state[key] = kept, swap(sent, "dp", orders[key[0]][n])
        kept, got = zip(*(state[key] for key in sorted(state)))
        own = call(
            functools.partial(turn_own, rows["end"], rows["pair"]), "turn_own", [struct((capacity, side, side), F32)],
            [VMEM] * (1 + len(kept)), [table, *kept],
        )[0]
        return own, *got

    operands = (table, slope, other_chosen, other_up, grad)
    ends = reduce(load_of, *operands)
    ends = lax.cond(table[rows["fits"], 0] == 1, lambda ends, operands: ends, lambda ends, operands: reduce(most_of, *operands), ends, operands)
    return call(
        functools.partial(finish, rows["end"], rows["pair"]), "finish", [struct((1, capacity, side, side), F32)],
        [VMEM] * (1 + len(ends)), [table, *ends],
    )[0]


def solution(mesh):
    return jax.shard_map(
        local,
        mesh=mesh,
        in_specs=(
            P("dp", "tensor"),
            P("dp", "tensor"),
            P("tensor", "dp", None, None),
            P("tensor", None),
            P("tensor", None),
            P("tensor", None),
        ),
        out_specs=P("tensor", "dp", None, None),
        check_vma=False,
    )
```
